32 devices in a mesh: seq: 32 (over z, y, x, core), rep: 1.
Axes of the slice: x: 2, y: 2, z: 4, core: 2. Of those that a mesh axis runs over, the one named last changes fastest.
Arguments:
- queries: bfloat16 [1, 4096, 2048], P('rep', 'seq'), may hold values from -9 to 9
- keys: bfloat16 [1, 4096, 512], P('rep', 'seq'), may hold values from -9 to 9
- values: bfloat16 [1, 4096, 512], P('rep', 'seq'), may hold values from -6 to 6
- conv_taps: float32 [4, 512], replicated, may hold values from -2 to 2
- grad_out: bfloat16 [1, 4096, 2048], P('rep', 'seq'), may hold values from -24 to 24
Outputs:
- grad_queries: bfloat16 [1, 4096, 2048], P('rep', 'seq')
- grad_keys: bfloat16 [1, 4096, 512], P('rep', 'seq')
- grad_values: bfloat16 [1, 4096, 512], P('rep', 'seq')
- grad_taps: float32 [2048], P('seq')
The draws below stay inside these ranges and needn't reach their ends.
All inputs are finite; a program needn't handle non-finite values.
Results may differ from the reference program's by a relative error of at most 0.012.
Values may be sent and summed in bfloat16 or wider, within the bound.
No kernel may reach another device: no remote copies, remote signals or barrier semaphores. Data moves between devices by JAX's collectives and lax.ppermute only.
A program may use at most 64 MiB of HBM per device.

```python
import math
import jax
import jax.numpy as jnp
from jax import lax

HEAD_SIZE = 128
QUERY_HEADS = 16
KEY_VALUE_HEADS = 4
TAPS = 4
TOK_DEV = 128
WINDOW = 1024
ROLLOUT_COUNT = 1
ROLLOUT_LENGTH = 4096
KVW = 512


def draw_queries(key, part):
    base_key = jax.random.fold_in(key, 11)
    array_shape = (ROLLOUT_COUNT, ROLLOUT_LENGTH, QUERY_HEADS * HEAD_SIZE)
    drawn = jnp.clip(jax.random.normal(base_key, array_shape, jnp.float32), -6.0, 6.0)
    return drawn.astype(jnp.bfloat16)


def draw_keys(key, part):
    base_key = jax.random.fold_in(key, 23)
    array_shape = (ROLLOUT_COUNT, ROLLOUT_LENGTH, KEY_VALUE_HEADS * HEAD_SIZE)
    drawn = jnp.clip(jax.random.normal(base_key, array_shape, jnp.float32), -6.0, 6.0)
    return drawn.astype(jnp.bfloat16)


def draw_grad_out(key, part):
    array_shape = (ROLLOUT_COUNT, ROLLOUT_LENGTH, QUERY_HEADS * HEAD_SIZE)
    noise_key = jax.random.fold_in(key, 31)
    positions = jnp.arange(ROLLOUT_LENGTH).astype(jnp.float32)
    rising = 1.0 + 2.0 * positions / float(ROLLOUT_LENGTH - 1)
    drawn = jnp.clip(jax.random.normal(noise_key, array_shape, jnp.float32), -4.0, 4.0)
    drawn = drawn * rising[None, :, None]
    return jnp.clip(drawn, -24.0, 24.0).astype(jnp.bfloat16)


def level_of(key, shape, shards, least, top_value):
    level = 1.0
    for axis_at, parts in shards:
        steps = jax.random.uniform(jax.random.fold_in(jax.random.fold_in(key, 6), axis_at), (parts,), jnp.float32, least / len(shards), top_value / len(shards))
        level = level * jnp.repeat(jnp.exp(steps), shape[axis_at] // parts).reshape((-1,) + (1,) * (len(shape) - 1 - axis_at))
    return level


def scatter_about(rng, shape, deviation, limit, split=(), held_as=jnp.bfloat16):
    drawn = deviation * jax.random.normal(rng, shape, jnp.float32)
    if split:
        drawn = drawn * level_of(rng, shape, split, -0.22, 0.18)
    return jnp.clip(drawn, -limit, limit).astype(held_as)


def setup_inputs(seed: int = 0) -> dict:
    key_of = jax.random.split(jax.random.key(seed), 6)
    return {
        "queries": draw_queries(jax.random.fold_in(key_of[5], 71), 0),
        "keys": draw_keys(jax.random.fold_in(key_of[5], 71), 0),
        "values": scatter_about(key_of[2], (ROLLOUT_COUNT, ROLLOUT_LENGTH, KVW), 1.0, 6.0, ((1, 32),)),
        "conv_taps": scatter_about(key_of[3], (TAPS, KVW), 0.5, 2.0, (), jnp.float32),
        "grad_out": draw_grad_out(jax.random.fold_in(key_of[5], 71), 0),
    }


NEG_FILL = -1e+30

def attend(query_block, grad_block, key_block, value_block, first_query, window):
    tok_rows = query_block.shape[0]
    keys_len = key_block.shape[0]
    kv_heads = key_block.shape[1] // HEAD_SIZE
    group_size = query_block.shape[1] // (HEAD_SIZE * kv_heads)
    inv_root = 1.0 / math.sqrt(HEAD_SIZE)
    query_pos = first_query + jnp.arange(tok_rows, dtype=jnp.int32)
    key_pos = first_query - window + jnp.arange(keys_len, dtype=jnp.int32)
    offset = query_pos[:, None] - key_pos[None, :]
    visible = (offset >= 0) & (offset < window) & (key_pos[None, :] >= 0)
    queries_grouped = query_block.reshape(tok_rows, kv_heads, group_size * HEAD_SIZE).transpose(1, 0, 2)
    grads_grouped = grad_block.reshape(tok_rows, kv_heads, group_size * HEAD_SIZE).transpose(1, 0, 2)
    keys_grouped = key_block.reshape(keys_len, kv_heads, HEAD_SIZE).transpose(1, 0, 2)
    values_grouped = value_block.reshape(keys_len, kv_heads, HEAD_SIZE).transpose(1, 0, 2)

    def one_group(operands):
        query_head, grad_head, key_head, value_head = operands
        query_head = query_head.reshape(tok_rows, group_size, HEAD_SIZE).astype(jnp.float32)
        grad_head = grad_head.reshape(tok_rows, group_size, HEAD_SIZE).astype(jnp.float32)
        key_wide = key_head.astype(jnp.float32)
        value_wide = value_head.astype(jnp.float32)
        scores = jnp.einsum('tgd,ld->gtl', query_head, key_wide) * inv_root
        scores = jnp.where(visible[None], scores, NEG_FILL)
        row_max = lax.optimization_barrier(jnp.max(scores, axis=-1, keepdims=True))
        row_sum = lax.optimization_barrier(jnp.sum(jnp.exp(scores - row_max), axis=-1, keepdims=True))
        log_total = row_max + jnp.log(row_sum)
        attn_prob = jnp.exp(scores - log_total)
        prob_low = attn_prob.astype(jnp.bfloat16)
        grad_prob = jnp.einsum('tgd,ld->gtl', grad_head, value_wide)
        row_delta = lax.optimization_barrier(jnp.sum(attn_prob * grad_prob, axis=-1, keepdims=True))
        grad_score = (attn_prob * (grad_prob - row_delta) * inv_root).astype(jnp.bfloat16)
        score_wide = grad_score.astype(jnp.float32)
        grad_query = jnp.einsum('gtl,ld->tgd', score_wide, key_wide).reshape(tok_rows, group_size * HEAD_SIZE)
        grad_key = jnp.einsum('gtl,tgd->ld', score_wide, query_head)
        grad_value = jnp.einsum('gtl,tgd->ld', prob_low.astype(jnp.float32), grad_head)
        return (grad_query, grad_key, grad_value)
    grad_query, grad_key, grad_value = lax.map(one_group, (queries_grouped, grads_grouped, keys_grouped, values_grouped))
    grad_query = grad_query.transpose(1, 0, 2).reshape(tok_rows, kv_heads * group_size * HEAD_SIZE)
    grad_key = grad_key.transpose(1, 0, 2).reshape(keys_len, kv_heads * HEAD_SIZE)
    grad_value = grad_value.transpose(1, 0, 2).reshape(keys_len, kv_heads * HEAD_SIZE)
    return (grad_query, grad_key, grad_value)

def reference(queries, keys, values, conv_taps, grad_out):
    seqs_count = queries.shape[0]
    rollout = queries.shape[1]
    kv_width = keys.shape[2]
    tap_count = conv_taps.shape[0]
    block_count = rollout // TOK_DEV

    def one_sequence(operands):
        query_seq, key_seq, value_seq, grad_seq = operands
        value_pad = jnp.pad(value_seq.astype(jnp.float32), ((tap_count - 1, 0), (0, 0)))
        summed = jnp.zeros((rollout, kv_width), jnp.float32)
        for index_k in range(tap_count):
            begin = tap_count - 1 - index_k
            summed = summed + conv_taps[index_k] * value_pad[begin:begin + rollout]
        mixed = summed.astype(jnp.bfloat16)
        key_pad = jnp.pad(key_seq, ((WINDOW, 0), (0, 0)))
        mixed_pad = jnp.pad(mixed, ((WINDOW, 0), (0, 0)))

        def one_block(carry, block_id):
            grad_keys_acc, grad_mixed_acc = carry
            start = (block_id * TOK_DEV).astype(jnp.int32)
            query_block = lax.dynamic_slice_in_dim(query_seq, start, TOK_DEV, 0)
            grad_block = lax.dynamic_slice_in_dim(grad_seq, start, TOK_DEV, 0)
            key_block = lax.dynamic_slice_in_dim(key_pad, start, WINDOW + TOK_DEV, 0)
            value_block = lax.dynamic_slice_in_dim(mixed_pad, start, WINDOW + TOK_DEV, 0)
            grad_query, grad_key, grad_value = attend(query_block, grad_block, key_block, value_block, start, WINDOW)
            old_keys = lax.dynamic_slice_in_dim(grad_keys_acc, start, WINDOW + TOK_DEV, 0)
            grad_keys_acc = lax.dynamic_update_slice_in_dim(grad_keys_acc, old_keys + grad_key, start, 0)
            old_mixed = lax.dynamic_slice_in_dim(grad_mixed_acc, start, WINDOW + TOK_DEV, 0)
            grad_mixed_acc = lax.dynamic_update_slice_in_dim(grad_mixed_acc, old_mixed + grad_value, start, 0)
            return ((grad_keys_acc, grad_mixed_acc), grad_query.astype(jnp.bfloat16))
        zeros_init = jnp.zeros((rollout + WINDOW, kv_width), jnp.float32)
        (grad_keys_acc, grad_mixed_acc), query_blocks = lax.scan(one_block, (zeros_init, zeros_init), jnp.arange(block_count, dtype=jnp.int32))
        grad_keys_seq = grad_keys_acc[WINDOW:]
        grad_mixed = grad_mixed_acc[WINDOW:]
        grad_pad = jnp.pad(grad_mixed, ((0, tap_count - 1), (0, 0)))
        grad_values_seq = jnp.zeros((rollout, kv_width), jnp.float32)
        tap_rows = []
        for index_k in range(tap_count):
            grad_values_seq = grad_values_seq + conv_taps[index_k] * grad_pad[index_k:index_k + rollout]
            begin = tap_count - 1 - index_k
            tap_rows.append(lax.optimization_barrier(jnp.sum(grad_mixed * value_pad[begin:begin + rollout], axis=0)))
        return (query_blocks.reshape(rollout, -1), grad_keys_seq.astype(jnp.bfloat16), grad_values_seq.astype(jnp.bfloat16), jnp.stack(tap_rows, axis=0))
    grad_queries, grad_keys, grad_values, tap_parts = lax.map(one_sequence, (queries, keys, values, grad_out))
    grad_taps = lax.optimization_barrier(jnp.sum(tap_parts, axis=0)).reshape(-1) / math.sqrt(seqs_count * rollout)
    return (grad_queries, grad_keys, grad_values, grad_taps)
```

```python
import functools
import math

import jax
import jax.numpy as jnp
from jax import lax
from jax.experimental import pallas as pl
from jax.experimental.pallas import tpu as pltpu
from jax.sharding import PartitionSpec as P

HEAD_SIZE = 128
WINDOW = 1024
NEG_FILL = -1e30
HALO = 16
VMEM_BYTES = 56 * 1024 * 1024


def passed_along(block, axis, distance):
    devices = range(lax.axis_size(axis))
    route = [(i - distance, i) for i in devices if i - distance in devices]
    return lax.ppermute(block, axis, route)


def whole(memory_space=pltpu.VMEM):
    return pl.BlockSpec(memory_space=memory_space)


def call(kernel, out_shape, operands, scratch=(), flops=0, smem=()):
    byte_count = sum(a.size * a.dtype.itemsize for a in operands)
    byte_count += sum(math.prod(o.shape) * o.dtype.itemsize for o in jax.tree.leaves(out_shape))
    specs = [whole(pltpu.SMEM if i in smem else pltpu.VMEM) for i in range(len(operands))]
    return pl.pallas_call(
        kernel,
        out_shape=out_shape,
        in_specs=specs,
        out_specs=jax.tree.map(lambda _: whole(), out_shape),
        scratch_shapes=list(scratch),
        cost_estimate=pl.CostEstimate(flops=flops, bytes_accessed=byte_count, transcendentals=0),
        compiler_params=pltpu.CompilerParams(vmem_limit_bytes=VMEM_BYTES),
    )(*operands)


def pack_kernel(group, queries, grad_out, keys, values, halo, taps, packed):
    rows = queries.shape[0]
    tap_count = taps.shape[0]
    width = queries.shape[1] // group
    extended = jnp.concatenate([halo[...], values[...]], axis=0).astype(jnp.float32)
    mixed = jnp.zeros(values.shape, jnp.float32)
    for index_k in range(tap_count):
        begin = HALO - index_k
        mixed = mixed + taps[index_k : index_k + 1, :] * extended[begin : begin + rows]
    mixed = mixed.astype(jnp.bfloat16)
    kv_heads = keys.shape[1] // HEAD_SIZE
    for member in range(group):
        head = slice((member * kv_heads // group) * HEAD_SIZE, (member * kv_heads // group + 1) * HEAD_SIZE)
        own = slice(member * width, (member + 1) * width)
        packed[member, :, 0:width] = queries[:, own]
        packed[member, :, width : 2 * width] = grad_out[:, own]
        packed[member, :, 2 * width : 2 * width + HEAD_SIZE] = keys[:, head]
        packed[member, :, 2 * width + HEAD_SIZE :] = mixed[:, head]


NT = (((1,), (1,)), ((), ()))
TN = (((0,), (0,)), ((), ()))
BLOCK = 256


def attend_kernel(has_before, own, before, grad_q, grad_kv, grad_before, key_all, mix_all, key_t, dkey, dmix):
    length = own.shape[0]
    width = grad_q.shape[1]
    heads = width // HEAD_SIZE
    blocks = length // BLOCK
    inv_root = 1.0 / math.sqrt(HEAD_SIZE)
    log2_scale = inv_root * math.log2(math.e)
    key_all[:length] = before[:, :HEAD_SIZE]
    mix_all[:length] = before[:, HEAD_SIZE:]
    key_all[length:] = own[:, 2 * width : 2 * width + HEAD_SIZE]
    mix_all[length:] = own[:, 2 * width + HEAD_SIZE :]
    key_t[...] = jnp.transpose(key_all[...])
    dkey[...] = jnp.zeros_like(dkey)
    dmix[...] = jnp.zeros_like(dmix)
    fill = jnp.where(has_before[0] == 0, NEG_FILL, 0.0).astype(jnp.float32)
    key_at = lax.broadcasted_iota(jnp.int32, (BLOCK, BLOCK), 0)
    query_at = lax.broadcasted_iota(jnp.int32, (BLOCK, BLOCK), 1)
    causal = key_at <= query_at

    @pl.loop(0, blocks)
    def _(step):
        first = pl.multiple_of(step * BLOCK, BLOCK)
        for head in range(heads):
            columns = slice(head * HEAD_SIZE, (head + 1) * HEAD_SIZE)
            grad_columns = slice(width + head * HEAD_SIZE, width + (head + 1) * HEAD_SIZE)
            query = own[pl.ds(first, BLOCK), columns]
            grad = own[pl.ds(first, BLOCK), grad_columns]

            def at(index):
                return pl.ds(pl.multiple_of(first + index * BLOCK, BLOCK), BLOCK)

            scores = [
                lax.dot_general(key_all[at(c), :], query, NT, preferred_element_type=jnp.float32)
                for c in range(blocks + 1)
            ]
            scores = [jnp.where(causal, scores[blocks], scores[0] + fill)] + scores[1:blocks]
            fills = [jnp.float32(0.0)] + [
                jnp.where(step + c < blocks, fill, 0.0) for c in range(1, blocks)
            ]
            peak = functools.reduce(
                jnp.maximum,
                [jnp.max(s, axis=0, keepdims=True) + f for s, f in zip(scores, fills)],
            )
            peak = peak * log2_scale
            probs = [jnp.exp2(s * log2_scale + (f - peak)) for s, f in zip(scores, fills)]
            total = functools.reduce(jnp.add, [jnp.sum(p, axis=0, keepdims=True) for p in probs])
            inverse = 1.0 / total
            grads = [
                lax.dot_general(mix_all[at(c), :], grad, NT, preferred_element_type=jnp.float32)
                for c in range(blocks + 1)
            ]
            grads = [jnp.where(causal, grads[blocks], grads[0])] + grads[1:blocks]
            probs = [p * inverse for p in probs]
            delta = functools.reduce(
                jnp.add, [jnp.sum(p * g, axis=0, keepdims=True) for p, g in zip(probs, grads)]
            )
            low = [p.astype(jnp.bfloat16) for p in probs]
            score_grads = [(p * (g - delta)).astype(jnp.bfloat16) for p, g in zip(probs, grads)]
            zero = jnp.zeros((), jnp.bfloat16)
            low = [jnp.where(causal, zero, low[0])] + low[1:] + [jnp.where(causal, low[0], zero)]
            score_grads = (
                [jnp.where(causal, zero, score_grads[0])]
                + score_grads[1:]
                + [jnp.where(causal, score_grads[0], zero)]
            )
            dquery_t = jnp.zeros((HEAD_SIZE, BLOCK), jnp.float32)
            for c in range(blocks + 1):
                dmix[at(c), :] += jnp.dot(low[c], grad, preferred_element_type=jnp.float32)
                dkey[at(c), :] += jnp.dot(score_grads[c], query, preferred_element_type=jnp.float32)
                dquery_t += jnp.dot(
                    key_t[:, at(c)], score_grads[c], preferred_element_type=jnp.float32
                )
            grad_q[pl.ds(first, BLOCK), columns] = (jnp.transpose(dquery_t) * inv_root).astype(jnp.bfloat16)

    grad_before[:, :HEAD_SIZE] = (dkey[:length] * inv_root).astype(jnp.bfloat16)
    grad_before[:, HEAD_SIZE:] = dmix[:length].astype(jnp.bfloat16)
    grad_kv[:, :HEAD_SIZE] = dkey[length:] * inv_root
    grad_kv[:, HEAD_SIZE:] = dmix[length:]


def unpack_kernel(group, received, grad_keys, grad_mixed):
    kv_heads = grad_keys.shape[1] // HEAD_SIZE
    share = group // kv_heads
    for head in range(kv_heads):
        total = received[head * share].astype(jnp.float32)
        for other in range(1, share):
            total = total + received[head * share + other].astype(jnp.float32)
        columns = slice(head * HEAD_SIZE, (head + 1) * HEAD_SIZE)
        grad_keys[:, columns] = total[:, :HEAD_SIZE].astype(jnp.bfloat16)
        grad_mixed[:, columns] = total[:, HEAD_SIZE:]


def finish_kernel(scale, grad_mixed, after, values, halo, taps, grad_values, tap_grads):
    rows = values.shape[0]
    tap_count = taps.shape[0]
    grad = grad_mixed[...]
    grad_ext = jnp.concatenate([grad, after[...]], axis=0)
    value_ext = jnp.concatenate([halo[...], values[...]], axis=0).astype(jnp.float32)
    total = jnp.zeros(values.shape, jnp.float32)
    for index_k in range(tap_count):
        total = total + taps[index_k : index_k + 1, :] * grad_ext[index_k : index_k + rows]
        begin = HALO - index_k
        tap_grads[index_k : index_k + 1, :] = (
            jnp.sum(grad * value_ext[begin : begin + rows], axis=0, keepdims=True) * scale
        )
    grad_values[...] = total.astype(jnp.bfloat16)


def on_device(queries, keys, values, conv_taps, grad_out):
    rows, width = queries.shape[1:]
    kv_width = keys.shape[2]
    group = WINDOW // rows
    count = lax.axis_size("seq")
    own_width = width // group
    groups = [[g * group + i for i in range(group)] for g in range(count // group)]
    bf16, f32 = jnp.bfloat16, jnp.float32
    shape = jax.ShapeDtypeStruct
    value_rows = values[0]
    halo = passed_along(value_rows[rows - HALO :], "seq", 1)
    packed = call(
        functools.partial(pack_kernel, group),
        shape((group, rows, 2 * own_width + 2 * HEAD_SIZE), bf16),
        (queries[0], grad_out[0], keys[0], value_rows, halo, conv_taps),
    )
    own = lax.all_to_all(packed, "seq", 0, 0, axis_index_groups=groups, tiled=True)
    own = own.reshape(WINDOW, 2 * own_width + 2 * HEAD_SIZE)
    before = passed_along(own[:, 2 * own_width :], "seq", group)
    has_before = (lax.axis_index("seq") >= group).astype(jnp.int32)[None]
    grad_q, grad_kv, grad_before = call(
        attend_kernel,
        (
            shape((WINDOW, own_width), bf16),
            shape((WINDOW, 2 * HEAD_SIZE), f32),
            shape((WINDOW, 2 * HEAD_SIZE), bf16),
        ),
        (has_before, own, before),
        scratch=[
            pltpu.VMEM((2 * WINDOW, HEAD_SIZE), bf16),
            pltpu.VMEM((2 * WINDOW, HEAD_SIZE), bf16),
            pltpu.VMEM((HEAD_SIZE, 2 * WINDOW), bf16),
            pltpu.VMEM((2 * WINDOW, HEAD_SIZE), f32),
            pltpu.VMEM((2 * WINDOW, HEAD_SIZE), f32),
        ],
        flops=10 * WINDOW * (WINDOW + BLOCK) * own_width,
        smem=(0,),
    )
    returned = passed_along(grad_before, "seq", -group)
    grad_q = lax.all_to_all(
        grad_q.reshape(group, rows, own_width), "seq", 0, 0, axis_index_groups=groups, tiled=True
    )
    grad_kv = (grad_kv + returned).astype(bf16).reshape(group, rows, 2 * HEAD_SIZE)
    grad_kv = lax.all_to_all(grad_kv, "seq", 0, 0, axis_index_groups=groups, tiled=True)
    grad_queries = grad_q.transpose(1, 0, 2).reshape(rows, width)
    grad_keys, grad_mixed = call(
        functools.partial(unpack_kernel, group),
        (shape((rows, kv_width), bf16), shape((rows, kv_width), f32)),
        (grad_kv,),
    )
    after = passed_along(grad_mixed[:8], "seq", -1)
    total_tokens = rows * count * lax.axis_size("rep")
    grad_values, tap_grads = call(
        functools.partial(finish_kernel, 1.0 / math.sqrt(total_tokens)),
        (shape((rows, kv_width), bf16), shape(conv_taps.shape, f32)),
        (grad_mixed, after, value_rows, halo, conv_taps),
    )
    shares = lax.all_to_all(tap_grads.reshape(count, -1), "seq", 0, 0, tiled=True)
    grad_taps = lax.psum(jnp.sum(shares, axis=0), "rep")
    return grad_queries[None], grad_keys[None], grad_values[None], grad_taps


def solution(mesh):
    in_specs = (
        P("rep", "seq", None),
        P("rep", "seq", None),
        P("rep", "seq", None),
        P(),
        P("rep", "seq", None),
    )
    out_specs = (P("rep", "seq", None), P("rep", "seq", None), P("rep", "seq", None), P("seq"))
    return jax.shard_map(
        on_device, mesh=mesh, in_specs=in_specs, out_specs=out_specs, check_vma=False
    )
```

```python
import functools
import math

import jax
import jax.numpy as jnp
from jax import lax
from jax.experimental import pallas as pl
from jax.experimental.pallas import tpu as pltpu
from jax.sharding import PartitionSpec as P

HEAD_SIZE = 128
WINDOW = 1024
NEG_FILL = -1e30
HALO = 16
VMEM_BYTES = 56 * 1024 * 1024
NT = (((1,), (1,)), ((), ()))


def attend_kernel(
    place, query_grad, kv_same, kv_other, old_same, old_other, halo, all_taps,
    grad_q, send, keep, grad_halo, tap_grads,
    key_all, key_t, value_all, mix_all, dkey, dmix,
):
    blocks, rows = query_grad.shape[:2]
    width = grad_q.shape[2]
    span = 2 * blocks
    length = span * rows
    lanes = 2 * HEAD_SIZE
    tap_count = all_taps.shape[0]
    has_before, parity, head_at = place[0], place[1], place[2]
    taps = all_taps[:, pl.ds(pl.multiple_of(head_at * HEAD_SIZE, HEAD_SIZE), HEAD_SIZE)]
    inv_root = 1.0 / math.sqrt(HEAD_SIZE)
    log2_scale = inv_root * math.log2(math.e)

    def block(index, offset=0):
        return pl.ds(pl.multiple_of(index * rows, rows) + offset, rows)

    value_all[:HALO] = halo[...].astype(jnp.float32)
    for start, same, other in ((0, old_same, old_other), (span, kv_same, kv_other)):
        for index in range(blocks):
            for source, at in ((same, start + 2 * index + parity), (other, start + 2 * index + 1 - parity)):
                key_all[block(at)] = source[index, :, :HEAD_SIZE]
                value_all[block(at, HALO)] = source[index, :, HEAD_SIZE:].astype(jnp.float32)
    mixed = taps[0:1] * value_all[HALO:]
    for index_k in range(1, tap_count):
        mixed = mixed + taps[index_k : index_k + 1] * value_all[HALO - index_k : HALO - index_k + 2 * length]
    mix_all[...] = mixed.astype(jnp.bfloat16)
    key_t[...] = jnp.transpose(key_all[...])
    dkey[...] = jnp.zeros_like(dkey)
    dmix[...] = jnp.zeros_like(dmix)
    fill = jnp.where(has_before == 0, NEG_FILL, 0.0).astype(jnp.float32)
    key_at = lax.broadcasted_iota(jnp.int32, (rows, lanes), 0)
    query_at = lax.broadcasted_iota(jnp.int32, (rows, lanes), 1) & (rows - 1)
    causal = key_at <= query_at

    @pl.loop(0, blocks)
    def _(step):
        number = 2 * step + parity
        first = pl.multiple_of(number * rows, rows)
        seen = pl.ds(first, length + rows)
        seen_halo = pl.ds(first + HALO, length + rows)
        keys = key_all[seen]
        mix = mix_all[seen]
        keys_t = key_t[:, seen]
        for pair in range(width // lanes):

            def stacked(base):
                return jnp.concatenate(
                    [query_grad[step, :, base + h * HEAD_SIZE : base + (h + 1) * HEAD_SIZE] for h in range(2)], axis=0
                )

            query = stacked(pair * lanes)
            grad = stacked(width + pair * lanes)
            scores = lax.dot_general(keys, query, NT, preferred_element_type=jnp.float32)
            grads = lax.dot_general(mix, grad, NT, preferred_element_type=jnp.float32)

            def folded(array, extra):
                edge = jnp.where(causal, array[length:], array[:rows] + extra if extra is not None else array[:rows])
                return [edge] + [array[c * rows : (c + 1) * rows] for c in range(1, span)]

            scores = folded(scores, fill)
            grads = folded(grads, None)
            fills = [jnp.float32(0.0)] + [jnp.where(number + c < span, fill, 0.0) for c in range(1, span)]
            peak = functools.reduce(
                jnp.maximum, [jnp.max(s, axis=0, keepdims=True) + f for s, f in zip(scores, fills)]
            )
            peak = peak * log2_scale
            probs = [jnp.exp2(s * log2_scale + (f - peak)) for s, f in zip(scores, fills)]
            total = functools.reduce(jnp.add, [jnp.sum(p, axis=0, keepdims=True) for p in probs])
            inverse = 1.0 / total
            probs = [p * inverse for p in probs]
            delta = functools.reduce(
                jnp.add, [jnp.sum(p * g, axis=0, keepdims=True) for p, g in zip(probs, grads)]
            )

            def unfolded(parts):
                zero = jnp.zeros((), jnp.bfloat16)
                low = [p.astype(jnp.bfloat16) for p in parts]
                return jnp.concatenate(
                    [jnp.where(causal, zero, low[0])] + low[1:] + [jnp.where(causal, low[0], zero)], axis=0
                )

            low = unfolded(probs)
            score_grads = unfolded([p * (g - delta) for p, g in zip(probs, grads)])
            dmix[seen_halo] += jnp.dot(low, grad, preferred_element_type=jnp.float32)
            dkey[seen] += jnp.dot(score_grads, query, preferred_element_type=jnp.float32)
            dquery = jnp.dot(keys_t, score_grads, preferred_element_type=jnp.float32)
            dquery = (jnp.transpose(dquery) * inv_root).astype(jnp.bfloat16)
            for h in range(2):
                base = pair * lanes + h * HEAD_SIZE
                grad_q[step, :, base : base + HEAD_SIZE] = dquery[h * rows : (h + 1) * rows]

    def convolved(start, count):
        total = taps[0:1] * dmix[pl.ds(start, count)]
        for index_k in range(1, tap_count):
            total = total + taps[index_k : index_k + 1] * dmix[pl.ds(start + index_k, count)]
        return total

    grad_halo[...] = convolved(0, HALO)
    for index in range(span):
        for target, at in ((keep, 2 * index + parity), (send, 2 * index + 1 - parity)):
            target[index, :, :HEAD_SIZE] = (dkey[block(at)] * inv_root).astype(target.dtype)
            target[index, :, HEAD_SIZE:] = convolved(pl.multiple_of(at * rows, rows) + HALO, rows).astype(target.dtype)
    for index_k in range(tap_count):
        tap_grads[index_k : index_k + 1] = jnp.sum(
            dmix[HALO : HALO + 2 * length] * value_all[HALO - index_k : HALO - index_k + 2 * length], axis=0, keepdims=True
        )


def on_device(queries, keys, values, conv_taps, grad_out):
    rows, width = queries.shape[1:]
    kv_width = keys.shape[2]
    tap_count = conv_taps.shape[0]
    kv_heads = kv_width // HEAD_SIZE
    group = WINDOW // rows
    share = group // kv_heads
    count = lax.axis_size("seq")
    planes = count // group
    own_width = width // kv_heads
    bf16, f32 = jnp.bfloat16, jnp.float32
    shape = jax.ShapeDtypeStruct
    device = lax.axis_index("seq")
    parity = device % share
    head_at = (device % group) // share
    same_core = [
        [g * group + j * share + c for j in range(kv_heads)] for g in range(planes) for c in range(share)
    ]
    across = [[g * group + p for g in range(planes)] for p in range(group)]

    def swap(array, groups):
        return lax.all_to_all(array, "seq", 0, 0, axis_index_groups=groups, tiled=True)

    def shifted(array, distance):
        route = [(i, i + distance) for i in range(count) if 0 <= i + distance < count]
        return lax.ppermute(array, "seq", route)

    def on_chip(array):
        return lax.ppermute(array, "seq", [(i, i ^ 1) for i in range(count)])

    def by_head(array):
        return array.reshape(rows, kv_heads, -1).transpose(1, 0, 2)

    kv_same = swap(jnp.concatenate([by_head(keys[0]), by_head(values[0])], axis=2), same_core)
    query_grad = swap(jnp.concatenate([by_head(queries[0]), by_head(grad_out[0])], axis=2), same_core)
    old_same = shifted(kv_same, group)
    kv_other = on_chip(kv_same)
    reach = 2 * group - (share - 1)
    halo = lax.ppermute(
        kv_same[kv_heads - 1, rows - HALO :, HEAD_SIZE:],
        "seq",
        [(i - reach, i) for i in range(count) if i % share == 0 and i - reach >= 0],
    )
    old_other = on_chip(old_same)
    place = jnp.stack([(device >= group).astype(jnp.int32), parity, head_at])
    span = 2 * kv_heads
    operands = (place, query_grad, kv_same, kv_other, old_same, old_other, halo, conv_taps)
    vmem = pl.BlockSpec(memory_space=pltpu.VMEM)
    grad_q, send, keep, grad_halo, tap_grads = pl.pallas_call(
        attend_kernel,
        out_shape=(
            shape((kv_heads, rows, own_width), bf16),
            shape((span, rows, 2 * HEAD_SIZE), bf16),
            shape((span, rows, 2 * HEAD_SIZE), f32),
            shape((HALO, HEAD_SIZE), f32),
            shape((tap_count, HEAD_SIZE), f32),
        ),
        in_specs=[pl.BlockSpec(memory_space=pltpu.SMEM)] + [vmem] * 7,
        out_specs=(vmem,) * 5,
        scratch_shapes=[
            pltpu.VMEM((2 * WINDOW, HEAD_SIZE), bf16),
            pltpu.VMEM((HEAD_SIZE, 2 * WINDOW), bf16),
            pltpu.VMEM((HALO + 2 * WINDOW, HEAD_SIZE), f32),
            pltpu.VMEM((2 * WINDOW, HEAD_SIZE), bf16),
            pltpu.VMEM((2 * WINDOW, HEAD_SIZE), f32),
            pltpu.VMEM((HALO + 2 * WINDOW + HALO, HEAD_SIZE), f32),
        ],
        cost_estimate=pl.CostEstimate(
            flops=10 * kv_heads * rows * (WINDOW + rows) * own_width, bytes_accessed=5 << 20, transcendentals=0
        ),
        compiler_params=pltpu.CompilerParams(vmem_limit_bytes=VMEM_BYTES),
    )(*operands)
    partial = keep + on_chip(send).astype(f32)
    returned = shifted(partial[:kv_heads].astype(bf16), -group)
    grad_queries = swap(grad_q, same_core).transpose(1, 0, 2).reshape(rows, width)
    returned_halo = lax.ppermute(
        grad_halo, "seq", [(i, i - reach) for i in range(count) if i % share == 0 and i - reach >= 0]
    )
    total = partial[kv_heads:] + returned.astype(f32)
    total = total.at[kv_heads - 1, rows - HALO :, HEAD_SIZE:].add(returned_halo)
    total = swap(total.astype(bf16), same_core).transpose(1, 0, 2)
    grad_keys = total[:, :, :HEAD_SIZE].reshape(rows, kv_width)
    grad_values = total[:, :, HEAD_SIZE:].reshape(rows, kv_width)
    tap_grads = tap_grads * (1.0 / math.sqrt(rows * count * lax.axis_size("rep")))
    if planes == tap_count and share == 2:
        own_tap = jnp.sum(swap(tap_grads, across), axis=0).reshape(share, -1)
        mine = jnp.where(parity == 0, own_tap[0], own_tap[1])
        theirs = jnp.where(parity == 0, own_tap[1], own_tap[0])
        grad_taps = mine + on_chip(theirs)
    else:
        spread = jnp.zeros((tap_count, kv_width), f32)
        spread = lax.dynamic_update_slice(spread, tap_grads, (0, head_at * HEAD_SIZE))
        grad_taps = jnp.sum(swap(spread.reshape(count, -1), None), axis=0)
    grad_taps = lax.psum(grad_taps, "rep")
    return grad_queries[None], grad_keys[None], grad_values[None], grad_taps


def solution(mesh):
    in_specs = (
        P("rep", "seq", None),
        P("rep", "seq", None),
        P("rep", "seq", None),
        P(),
        P("rep", "seq", None),
    )
    out_specs = (P("rep", "seq", None), P("rep", "seq", None), P("rep", "seq", None), P("seq"))
    return jax.shard_map(
        on_device, mesh=mesh, in_specs=in_specs, out_specs=out_specs, check_vma=False
    )
```

```python
import math

import jax
import jax.numpy as jnp
from jax import lax
from jax.experimental import pallas as pl
from jax.experimental.pallas import tpu as pltpu
from jax.sharding import PartitionSpec as P

HEAD_SIZE = 128
WINDOW = 1024
NEG_FILL = -1e30
HALO = 16
VMEM_BYTES = 56 * 1024 * 1024
NT = (((1,), (1,)), ((), ()))


def run(kernel, out_shape, operands, scratch=(), flops=0):
    vmem = pl.BlockSpec(memory_space=pltpu.VMEM)
    moved = list(operands) + list(out_shape)
    return pl.pallas_call(
        kernel,
        out_shape=out_shape,
        in_specs=[pl.BlockSpec(memory_space=pltpu.SMEM)] + [vmem] * (len(operands) - 1),
        out_specs=[vmem] * len(out_shape),
        scratch_shapes=list(scratch),
        cost_estimate=pl.CostEstimate(
            flops=flops, bytes_accessed=sum(math.prod(a.shape) * a.dtype.itemsize for a in moved), transcendentals=0
        ),
        compiler_params=pltpu.CompilerParams(vmem_limit_bytes=VMEM_BYTES),
    )(*operands)


def columns_of(index):
    return pl.ds(pl.multiple_of(index * HEAD_SIZE, HEAD_SIZE), HEAD_SIZE)


def pack_kernel(place, queries, grad_out, keys, values, packed, *parts):
    head_at = place[2]
    heads, _, width = packed.shape
    for head in range(heads):
        own = slice(head * (width // 2), (head + 1) * (width // 2))
        packed[head, :, : width // 2] = queries[:, own]
        packed[head, :, width // 2 :] = grad_out[:, own]
    for turn, part in enumerate(parts):
        at = columns_of(head_at ^ turn)
        part[:, :HEAD_SIZE] = keys[:, at]
        part[:, HEAD_SIZE:] = values[:, at]


def unpack_kernel(place, *refs):
    parts, (grad_keys, grad_values) = refs[:-2], refs[-2:]
    head_at = place[2]
    for turn, part in enumerate(parts):
        at = columns_of(head_at ^ turn)
        grad_keys[:, at] = part[:, :HEAD_SIZE]
        grad_values[:, at] = part[:, HEAD_SIZE:]


def prepare_kernel(
    place, kv_same, kv_other, old_same, old_other, halo, all_taps, key_all, key_t, mix_all, value_all
):
    blocks, rows = kv_same.shape[:2]
    span = 2 * blocks
    tap_count = all_taps.shape[0]
    parity, head_at = place[1], place[2]
    taps = all_taps[:, columns_of(head_at)]
    value_all[:HALO] = halo[...].astype(jnp.float32)
    for start, same, other in ((0, old_same, old_other), (span, kv_same, kv_other)):
        for turn in range(blocks):
            for source, core in ((same, parity), (other, 1 - parity)):
                first = (start + 2 * (head_at ^ turn) + core) * rows
                first = pl.multiple_of(first, rows)
                key_all[pl.ds(first, rows)] = source[turn, :, :HEAD_SIZE]
                value_all[pl.ds(first + HALO, rows)] = source[turn, :, HEAD_SIZE:].astype(jnp.float32)
    for start in range(HALO, HALO + 2 * span * rows, rows):
        mixed = taps[0:1] * value_all[start : start + rows]
        for index_k in range(1, tap_count):
            mixed = mixed + taps[index_k : index_k + 1] * value_all[start - index_k : start - index_k + rows]
        mix_all[start - HALO : start - HALO + rows] = mixed.astype(jnp.bfloat16)
    key_t[...] = jnp.transpose(key_all[...])


def attend_kernel(
    place, query_grad, key_all, key_t, mix_all, all_taps,
    grad_q, send_old, send_own, keep_old, keep_own, grad_halo, dmix,
    dkey, *work,
):
    blocks, rows = query_grad.shape[:2]
    width = grad_q.shape[2]
    span = 2 * blocks
    length = span * rows
    lanes = 2 * HEAD_SIZE
    pairs = width // lanes
    tap_count = all_taps.shape[0]
    has_before, parity, head_at = place[0], place[1], place[2]
    taps = all_taps[:, columns_of(head_at)]
    inv_root = 1.0 / math.sqrt(HEAD_SIZE)
    log2_scale = inv_root * math.log2(math.e)
    score_refs, gprob_refs, low_refs, dscore_refs = work[0:2], work[2:4], work[4:6], work[6:8]
    dkey[...] = jnp.zeros_like(dkey)
    dmix[...] = jnp.zeros_like(dmix)
    fill = jnp.where(has_before == 0, NEG_FILL, 0.0).astype(jnp.float32)
    key_at = lax.broadcasted_iota(jnp.int32, (rows, lanes), 0)
    query_at = lax.broadcasted_iota(jnp.int32, (rows, lanes), 1) & (rows - 1)
    causal = key_at <= query_at
    stats = {}

    def places(n):
        step, pair = n // pairs, n % pairs
        number = 2 * step + parity
        return step, pair, number, pl.multiple_of(number * rows, rows)

    def stacked(step, base):
        return jnp.concatenate(
            [query_grad[step, :, base + h * HEAD_SIZE : base + (h + 1) * HEAD_SIZE] for h in range(2)], axis=0
        )

    def by_eight(array):
        return array.reshape(-1, 8, array.shape[1])

    def scores_stage(n):
        step, pair, number, first = places(n)
        seen = pl.ds(first, length + rows)
        scores = lax.dot_general(
            key_all[seen], stacked(step, pair * lanes), NT, preferred_element_type=jnp.float32
        )
        grads = lax.dot_general(
            mix_all[seen], stacked(step, width + pair * lanes), NT, preferred_element_type=jnp.float32
        )
        edge = jnp.where(causal, scores[length:], scores[:rows] + fill)
        score_refs[n % 2][:rows] = edge
        score_refs[n % 2][rows:] = scores[rows:length]
        gprob_refs[n % 2][:rows] = jnp.where(causal, grads[length:], grads[:rows])
        gprob_refs[n % 2][rows:] = grads[rows:length]
        peak = jnp.max(by_eight(edge), axis=0)
        for c in range(1, span):
            part = jnp.max(by_eight(scores[c * rows : (c + 1) * rows]), axis=0)
            peak = jnp.maximum(peak, part + jnp.where(number + c < span, fill, 0.0))
        stats[n] = jnp.max(peak, axis=0, keepdims=True) * log2_scale

    def softmax_stage(n):
        step, pair, number, first = places(n)
        peak = stats[n]
        scores, gprob, low, dscore = (refs[n % 2] for refs in (score_refs, gprob_refs, low_refs, dscore_refs))
        total = jnp.zeros((8, lanes), jnp.float32)
        delta = jnp.zeros((8, lanes), jnp.float32)
        for c in range(span):
            at = slice(c * rows, (c + 1) * rows)
            shift = -peak if c == 0 else jnp.where(number + c < span, fill, 0.0) - peak
            prob = jnp.exp2(scores[at] * log2_scale + shift)
            total = total + jnp.sum(by_eight(prob), axis=0)
            delta = delta + jnp.sum(by_eight(prob * gprob[at]), axis=0)
            low[at] = prob.astype(jnp.bfloat16)
        inverse = 1.0 / jnp.sum(total, axis=0, keepdims=True)
        delta = jnp.sum(delta, axis=0, keepdims=True) * inverse
        for c in range(span):
            at = slice(c * rows, (c + 1) * rows)
            dscore[at] = low[at] * (gprob[at] - delta).astype(jnp.bfloat16)
        zero = jnp.zeros((), jnp.bfloat16)
        for ref in (low, dscore):
            edge = ref[:rows]
            ref[length:] = jnp.where(causal, edge, zero)
            ref[:rows] = jnp.where(causal, zero, edge)
        stats[n] = inverse

    def gradient_stage(n):
        step, pair, number, first = places(n)
        seen = pl.ds(first, length + rows)
        inverse = stats[n]
        column = jnp.transpose(jnp.broadcast_to(inverse, (HEAD_SIZE, lanes)))
        query = (stacked(step, pair * lanes).astype(jnp.float32) * column).astype(jnp.bfloat16)
        grad = (stacked(step, width + pair * lanes).astype(jnp.float32) * column).astype(jnp.bfloat16)
        low, dscore = low_refs[n % 2], dscore_refs[n % 2]
        dmix[pl.ds(first + HALO, length + rows)] += jnp.dot(low[...], grad, preferred_element_type=jnp.float32)
        dkey[seen] += jnp.dot(dscore[...], query, preferred_element_type=jnp.float32)
        dquery = jnp.dot(key_t[:, seen], dscore[...], preferred_element_type=jnp.float32)
        dquery = jnp.transpose(dquery * (inverse * inv_root)).astype(jnp.bfloat16)
        for h in range(2):
            base = pair * lanes + h * HEAD_SIZE
            grad_q[step, :, base : base + HEAD_SIZE] = dquery[h * rows : (h + 1) * rows]

    count = blocks * pairs
    for n in range(count + 2):
        if n < count:
            scores_stage(n)
        if 1 <= n <= count:
            softmax_stage(n - 1)
        if n >= 2:
            gradient_stage(n - 2)

    def convolved(start, size):
        total = taps[0:1] * dmix[pl.ds(start, size)]
        for index_k in range(1, tap_count):
            total = total + taps[index_k : index_k + 1] * dmix[pl.ds(start + index_k, size)]
        return total

    grad_halo[...] = convolved(0, HALO)
    for start, keep, send in ((0, keep_old, send_old), (span, keep_own, send_own)):
        for turn in range(blocks):
            for target, core in ((keep, parity), (send, 1 - parity)):
                first = pl.multiple_of((start + 2 * (head_at ^ turn) + core) * rows, rows)
                target[turn, :, :HEAD_SIZE] = (dkey[pl.ds(first, rows)] * inv_root).astype(target.dtype)
                target[turn, :, HEAD_SIZE:] = convolved(first + HALO, rows).astype(target.dtype)


def taps_kernel(scale, place, dmix, value_all, tap_grads):
    tap_count = tap_grads.shape[0]
    rows = 128
    sums = [jnp.zeros((8, HEAD_SIZE), jnp.float32)] * tap_count
    for start in range(HALO, value_all.shape[0], rows):
        grad = dmix[start : start + rows]
        for index_k in range(tap_count):
            product = grad * value_all[start - index_k : start - index_k + rows]
            sums[index_k] = sums[index_k] + jnp.sum(product.reshape(-1, 8, HEAD_SIZE), axis=0)
    for index_k in range(tap_count):
        tap_grads[index_k : index_k + 1] = jnp.sum(sums[index_k], axis=0, keepdims=True) * scale


def on_device(queries, keys, values, conv_taps, grad_out):
    rows, width = queries.shape[1:]
    kv_width = keys.shape[2]
    tap_count = conv_taps.shape[0]
    kv_heads = kv_width // HEAD_SIZE
    group = WINDOW // rows
    share = group // kv_heads
    count = lax.axis_size("seq")
    planes = count // group
    own_width = width // kv_heads
    bf16, f32 = jnp.bfloat16, jnp.float32
    shape = jax.ShapeDtypeStruct
    device = lax.axis_index("seq")
    parity = device % share
    head_at = (device % group) // share
    plane = device // group
    same_core = [[g * group + j * share + c for j in range(kv_heads)] for g in range(planes) for c in range(share)]
    place = jnp.stack([(device >= group).astype(jnp.int32), parity, head_at, plane])

    def swap(array, groups):
        return lax.all_to_all(array, "seq", 0, 0, axis_index_groups=groups, tiled=True)

    def routed(array, distance, chosen=lambda i: True):
        route = [(i, i + distance) for i in range(count) if 0 <= i + distance < count and chosen(i)]
        return lax.ppermute(array, "seq", route)

    def flipped(array, bits):
        return lax.ppermute(array, "seq", [(i, i ^ bits) for i in range(count)])

    kv_shape = shape((rows, 2 * HEAD_SIZE), bf16)
    kv_blocks = (kv_heads, rows, 2 * HEAD_SIZE)
    packed, *parts = run(
        pack_kernel,
        [shape((kv_heads, rows, 2 * own_width), bf16)] + [kv_shape] * kv_heads,
        (place, queries[0], grad_out[0], keys[0], values[0]),
    )
    query_grad = swap(packed, same_core)
    kv_same = jnp.stack([parts[0]] + [flipped(parts[turn], turn * share) for turn in range(1, kv_heads)])
    old_same = routed(kv_same, group)
    kv_other = flipped(kv_same, 1)
    old_other = flipped(old_same, 1)
    last = lax.dynamic_index_in_dim(kv_same, head_at ^ (kv_heads - 1), 0, keepdims=False)
    reach = 2 * group - (share - 1)
    halo = routed(last[rows - HALO :, HEAD_SIZE:], reach, lambda i: i % share == share - 1)
    key_all, key_t, mix_all, value_all = run(
        prepare_kernel,
        [
            shape((2 * WINDOW, HEAD_SIZE), bf16),
            shape((HEAD_SIZE, 2 * WINDOW), bf16),
            shape((2 * WINDOW, HEAD_SIZE), bf16),
            shape((HALO + 2 * WINDOW, HEAD_SIZE), f32),
        ],
        (place, kv_same, kv_other, old_same, old_other, halo, conv_taps),
    )
    lanes = 2 * HEAD_SIZE
    grad_q, send_old, send_own, keep_old, keep_own, grad_halo, dmix = run(
        attend_kernel,
        [
            shape((kv_heads, rows, own_width), bf16),
            shape(kv_blocks, bf16),
            shape(kv_blocks, bf16),
            shape(kv_blocks, f32),
            shape(kv_blocks, f32),
            shape((HALO, HEAD_SIZE), f32),
            shape((HALO + 2 * WINDOW + HALO, HEAD_SIZE), f32),
        ],
        (place, query_grad, key_all, key_t, mix_all, conv_taps),
        scratch=[pltpu.VMEM((2 * WINDOW, HEAD_SIZE), f32)]
        + [pltpu.VMEM((WINDOW, lanes), f32)] * 4
        + [pltpu.VMEM((WINDOW + rows, lanes), bf16)] * 4,
        flops=10 * kv_heads * rows * (WINDOW + rows) * own_width,
    )
    returned = routed((keep_old + flipped(send_old, 1).astype(f32)).astype(bf16), -group)
    returned_halo = routed(grad_halo, -reach, lambda i: i % share == 0)
    grad_queries = swap(grad_q, same_core).transpose(1, 0, 2).reshape(rows, width)
    total = keep_own + flipped(send_own, 1).astype(f32) + returned.astype(f32)
    halo_block = jnp.pad(returned_halo, ((rows - HALO, 0), (HEAD_SIZE, 0)))
    owned = []
    for turn in range(kv_heads):
        mine = total[turn] + jnp.where((head_at ^ turn) == kv_heads - 1, halo_block, 0.0)
        owned.append(mine.astype(bf16))
    owned = [owned[0]] + [flipped(owned[turn], turn * share) for turn in range(1, kv_heads)]
    grad_keys, grad_values = run(
        unpack_kernel, [shape((rows, kv_width), bf16), shape((rows, kv_width), bf16)], (place, *owned)
    )
    scale = 1.0 / math.sqrt(rows * count * lax.axis_size("rep"))
    (tap_grads,) = run(
        lambda *refs: taps_kernel(scale, *refs), [shape((tap_count, HEAD_SIZE), f32)], (place, dmix, value_all)
    )
    if planes == tap_count == 4 and share == 2:
        for bits, bit in ((2 * group, plane // 2), (group, plane % 2)):
            half = tap_grads.shape[0] // 2
            low, high = tap_grads[:half], tap_grads[half:]
            tap_grads = jnp.where(bit == 0, low, high) + flipped(jnp.where(bit == 0, high, low), bits)
        low, high = jnp.split(tap_grads[0], 2)
        grad_taps = jnp.where(parity == 0, low, high) + flipped(jnp.where(parity == 0, high, low), 1)
    else:
        spread = jnp.zeros((tap_count, kv_width), f32)
        spread = lax.dynamic_update_slice(spread, tap_grads, (0, head_at * HEAD_SIZE))
        grad_taps = jnp.sum(swap(spread.reshape(count, -1), None), axis=0)
    grad_taps = lax.psum(grad_taps, "rep")
    return grad_queries[None], grad_keys[None], grad_values[None], grad_taps


def solution(mesh):
    in_specs = (
        P("rep", "seq", None),
        P("rep", "seq", None),
        P("rep", "seq", None),
        P(),
        P("rep", "seq", None),
    )
    out_specs = (P("rep", "seq", None), P("rep", "seq", None), P("rep", "seq", None), P("seq"))
    return jax.shard_map(
        on_device, mesh=mesh, in_specs=in_specs, out_specs=out_specs, check_vma=False
    )
```

```python
import functools
import math

import jax
import jax.numpy as jnp
from jax import lax
from jax.experimental import pallas as pl
from jax.experimental.pallas import tpu as pltpu
from jax.sharding import PartitionSpec as P

HEAD_SIZE = 128
WINDOW = 1024
NEG_FILL = -1e30
HALO = 16
VMEM_BYTES = 56 * 1024 * 1024
NT = (((1,), (1,)), ((), ()))


def place_of(group, share):
    device = lax.axis_index("seq")
    return lax.div(device, group), lax.rem(device, share), lax.div(lax.rem(device, group), share)


def run(kernel, out_shape, operands, scratch=(), flops=0):
    vmem = pl.BlockSpec(memory_space=pltpu.VMEM)
    moved = list(operands) + list(out_shape)
    return pl.pallas_call(
        kernel,
        out_shape=out_shape,
        in_specs=[vmem] * len(operands),
        out_specs=[vmem] * len(out_shape),
        scratch_shapes=list(scratch),
        cost_estimate=pl.CostEstimate(
            flops=flops, bytes_accessed=sum(math.prod(a.shape) * a.dtype.itemsize for a in moved), transcendentals=0
        ),
        compiler_params=pltpu.CompilerParams(vmem_limit_bytes=VMEM_BYTES),
    )(*operands)


def columns_of(index, width=HEAD_SIZE):
    return pl.ds(pl.multiple_of(index * width, HEAD_SIZE), width)


def pack_kernel(place, queries, grad_out, keys, values, *parts):
    rows = queries.shape[0]
    turns = len(parts) // 2
    heads = queries.shape[1] // HEAD_SIZE // turns
    for turn in range(turns):
        target = place[2] ^ turn
        part = parts[turn]
        part[:, :HEAD_SIZE] = keys[:, columns_of(target)]
        part[:, HEAD_SIZE:] = values[:, columns_of(target)]
        part = parts[turns + turn]
        for base, source in ((0, queries), (heads, grad_out)):
            for head in range(heads):
                at = slice((base + head) * rows, (base + head + 1) * rows)
                part[at] = source[:, columns_of(target * heads + head)]


def unpack_queries_kernel(place, *refs):
    parts, grad_queries = refs[:-1], refs[-1]
    for turn, part in enumerate(parts):
        grad_queries[:, columns_of(place[2] ^ turn, part.shape[1])] = part[...]


def unpack_kernel(place, *refs):
    parts, (grad_keys, grad_values) = refs[:-2], refs[-2:]
    head_at = place[2]
    for turn, part in enumerate(parts):
        at = columns_of(head_at ^ turn)
        grad_keys[:, at] = part[:, :HEAD_SIZE]
        grad_values[:, at] = part[:, HEAD_SIZE:]


def attend_kernel(scale, turns, place, *refs):
    kv_same, kv_other, old_same, old_other, halo, all_taps = refs[:6]
    query_grads = refs[6 : 6 + turns]
    grad_qs = refs[6 + turns : 6 + 2 * turns]
    send, keep_old, keep_own, tap_keep = refs[6 + 2 * turns : 10 + 2 * turns]
    key_all, key_t, value_all, mix_all, dkey, dmix, *work = refs[10 + 2 * turns :]
    rows, width = grad_qs[0].shape
    blocks = turns
    span = 2 * blocks
    length = span * rows
    lanes = 2 * HEAD_SIZE
    pairs = width // lanes
    tap_count = all_taps.shape[0]
    group_at, parity, head_at = place
    taps = all_taps[:, columns_of(head_at)]
    inv_root = 1.0 / math.sqrt(HEAD_SIZE)
    log2_scale = inv_root * math.log2(math.e)
    score_refs, gprob_refs, low_refs, dscore_refs = work[0:2], work[2:4], work[4:6], work[6:8]

    def block_at(turn, core):
        return 2 * (head_at ^ turn) + core

    value_all[:HALO] = halo[...].astype(jnp.float32)
    for start, same, other in ((0, old_same, old_other), (span, kv_same, kv_other)):
        for turn in range(blocks):
            for source, core in ((same, parity), (other, 1 - parity)):
                first = pl.multiple_of((start + block_at(turn, core)) * rows, rows)
                key_all[pl.ds(first, rows)] = source[turn, :, :HEAD_SIZE]
                value_all[pl.ds(first + HALO, rows)] = source[turn, :, HEAD_SIZE:].astype(jnp.float32)
    for start in range(HALO, HALO + 2 * length, rows):
        mixed = taps[0:1] * value_all[start : start + rows]
        for index_k in range(1, tap_count):
            mixed = mixed + taps[index_k : index_k + 1] * value_all[start - index_k : start - index_k + rows]
        mix_all[start - HALO : start - HALO + rows] = mixed.astype(jnp.bfloat16)
    key_t[...] = jnp.transpose(key_all[...])
    dkey[...] = jnp.zeros_like(dkey)
    dmix[...] = jnp.zeros_like(dmix)
    fill = jnp.where(group_at == 0, NEG_FILL, 0.0).astype(jnp.float32)
    key_at = lax.broadcasted_iota(jnp.int32, (rows, lanes), 0)
    query_at = lax.broadcasted_iota(jnp.int32, (rows, lanes), 1) & (rows - 1)
    causal = key_at <= query_at
    stats = {}

    def places(n):
        step, pair = n // pairs, n % pairs
        number = block_at(step, parity)
        return step, pair, number, pl.multiple_of(number * rows, rows)

    def stacked(step, base):
        return query_grads[step][base // HEAD_SIZE * rows : (base + lanes) // HEAD_SIZE * rows]

    def by_eight(array):
        return array.reshape(-1, 8, array.shape[1])

    def scores_stage(n):
        step, pair, number, first = places(n)
        seen = pl.ds(first, length + rows)
        scores = lax.dot_general(
            key_all[seen], stacked(step, pair * lanes), NT, preferred_element_type=jnp.float32
        )
        grads = lax.dot_general(
            mix_all[seen], stacked(step, width + pair * lanes), NT, preferred_element_type=jnp.float32
        )
        edge = jnp.where(causal, scores[length:], scores[:rows] + fill)
        score_refs[n % 2][:rows] = edge
        score_refs[n % 2][rows:] = scores[rows:length]
        gprob_refs[n % 2][:rows] = jnp.where(causal, grads[length:], grads[:rows])
        gprob_refs[n % 2][rows:] = grads[rows:length]
        peak = jnp.max(by_eight(edge), axis=0)
        for c in range(1, span):
            part = jnp.max(by_eight(scores[c * rows : (c + 1) * rows]), axis=0)
            peak = jnp.maximum(peak, part + jnp.where(number + c < span, fill, 0.0))
        stats[n] = jnp.max(peak, axis=0, keepdims=True) * log2_scale

    def softmax_stage(n):
        step, pair, number, first = places(n)
        peak = stats[n]
        scores, gprob, low, dscore = (refs[n % 2] for refs in (score_refs, gprob_refs, low_refs, dscore_refs))
        total = jnp.zeros((8, lanes), jnp.float32)
        delta = jnp.zeros((8, lanes), jnp.float32)
        for c in range(span):
            at = slice(c * rows, (c + 1) * rows)
            shift = -peak if c == 0 else jnp.where(number + c < span, fill, 0.0) - peak
            prob = jnp.exp2(scores[at] * log2_scale + shift)
            total = total + jnp.sum(by_eight(prob), axis=0)
            delta = delta + jnp.sum(by_eight(prob * gprob[at]), axis=0)
            low[at] = prob.astype(jnp.bfloat16)
        inverse = 1.0 / jnp.sum(total, axis=0, keepdims=True)
        delta = jnp.sum(delta, axis=0, keepdims=True) * inverse
        for c in range(span):
            at = slice(c * rows, (c + 1) * rows)
            dscore[at] = low[at] * (gprob[at] - delta).astype(jnp.bfloat16)
        zero = jnp.zeros((), jnp.bfloat16)
        for ref in (low, dscore):
            edge = ref[:rows]
            ref[length:] = jnp.where(causal, edge, zero)
            ref[:rows] = jnp.where(causal, zero, edge)
        stats[n] = inverse

    def gradient_stage(n):
        step, pair, number, first = places(n)
        seen = pl.ds(first, length + rows)
        inverse = stats[n]
        column = jnp.transpose(jnp.broadcast_to(inverse, (HEAD_SIZE, lanes)))
        query = (stacked(step, pair * lanes).astype(jnp.float32) * column).astype(jnp.bfloat16)
        grad = (stacked(step, width + pair * lanes).astype(jnp.float32) * column).astype(jnp.bfloat16)
        low, dscore = low_refs[n % 2], dscore_refs[n % 2]
        dmix[pl.ds(first + HALO, length + rows)] += jnp.dot(low[...], grad, preferred_element_type=jnp.float32)
        dkey[seen] += jnp.dot(dscore[...], query, preferred_element_type=jnp.float32)
        dquery = jnp.dot(key_t[:, seen], dscore[...], preferred_element_type=jnp.float32)
        dquery = jnp.transpose(dquery * (inverse * inv_root)).astype(jnp.bfloat16)
        for h in range(2):
            base = pair * lanes + h * HEAD_SIZE
            grad_qs[step][:, base : base + HEAD_SIZE] = dquery[h * rows : (h + 1) * rows]

    count = blocks * pairs
    for n in range(count + 2):
        if n < count:
            scores_stage(n)
        if 1 <= n <= count:
            softmax_stage(n - 1)
        if n >= 2:
            gradient_stage(n - 2)

    def convolved(start, size):
        total = taps[0:1] * dmix[pl.ds(start, size)]
        for index_k in range(1, tap_count):
            total = total + taps[index_k : index_k + 1] * dmix[pl.ds(start + index_k, size)]
        return total

    for start, keep, base in ((0, keep_old, 0), (span, keep_own, blocks * rows)):
        for turn in range(blocks):
            for target, core, offset in ((keep, parity, 0), (send, 1 - parity, base)):
                first = pl.multiple_of((start + block_at(turn, core)) * rows, rows)
                at = slice(offset + turn * rows, offset + (turn + 1) * rows)
                target[at, :HEAD_SIZE] = (dkey[pl.ds(first, rows)] * inv_root).astype(target.dtype)
                target[at, HEAD_SIZE:] = convolved(first + HALO, rows).astype(target.dtype)
    note = slice(2 * blocks * rows, 2 * blocks * rows + HALO)
    send[note, HEAD_SIZE:] = convolved(0, HALO).astype(send.dtype)
    sums = [jnp.zeros((8, HEAD_SIZE), jnp.float32)] * tap_count
    for start in range(HALO, HALO + 2 * length, rows):
        grad = dmix[start : start + rows]
        for index_k in range(tap_count):
            sums[index_k] = sums[index_k] + jnp.sum(
                by_eight(grad * value_all[start - index_k : start - index_k + rows]), axis=0
            )
    tap_grads = jnp.concatenate([jnp.sum(total, axis=0, keepdims=True) for total in sums], axis=0) * scale
    low, high = tap_grads[:, : HEAD_SIZE // 2], tap_grads[:, HEAD_SIZE // 2 :]
    tap_keep[...] = jnp.where(parity == 0, low, high)
    theirs = jnp.where(parity == 0, high, low)
    upper = theirs.astype(send.dtype).astype(jnp.float32)
    theirs = jnp.concatenate([upper, theirs - upper], axis=0)
    theirs = jnp.concatenate([theirs, jnp.zeros((HALO - 2 * tap_count, HEAD_SIZE // 2), jnp.float32)], axis=0)
    theirs = jnp.concatenate([theirs, jnp.zeros_like(theirs)], axis=1)
    send[note, :HEAD_SIZE] = theirs.astype(send.dtype)


def on_device(queries, keys, values, conv_taps, grad_out):
    rows, width = queries.shape[1:]
    kv_width = keys.shape[2]
    tap_count = conv_taps.shape[0]
    kv_heads = kv_width // HEAD_SIZE
    group = WINDOW // rows
    share = group // kv_heads
    count = lax.axis_size("seq")
    planes = count // group
    own_width = width // kv_heads
    bf16, f32 = jnp.bfloat16, jnp.float32
    shape = jax.ShapeDtypeStruct
    plane, parity, head_at = place_of(group, share)

    def launch(kernel, out_shape, operands, **options):
        return run(lambda *refs: kernel(place_of(group, share), *refs), out_shape, operands, **options)

    def routed(array, distance, chosen=lambda i: True):
        route = [(i, i + distance) for i in range(count) if 0 <= i + distance < count and chosen(i)]
        return lax.ppermute(array, "seq", route)

    def flipped(array, bits):
        return lax.ppermute(array, "seq", [(i, i ^ bits) for i in range(count)])

    def after(others, *arrays):
        return lax.optimization_barrier((*arrays, *others))[: len(arrays)]

    def exchanged(parts):
        return [parts[0]] + [flipped(parts[turn], turn * share) for turn in range(1, kv_heads)]

    kv_shape = shape((rows, 2 * HEAD_SIZE), bf16)
    query_shape = shape((2 * own_width // HEAD_SIZE * rows, HEAD_SIZE), bf16)
    parts = launch(
        pack_kernel,
        [kv_shape] * kv_heads + [query_shape] * kv_heads,
        (queries[0], grad_out[0], keys[0], values[0]),
    )
    kv_same = jnp.stack(exchanged(parts[:kv_heads]))
    old_same = routed(kv_same, group)
    query_grads = exchanged(after([kv_same], *parts[kv_heads:]))
    kv_same, old_same = lax.optimization_barrier((kv_same, old_same))
    old_other = flipped(old_same, 1)
    kv_other = flipped(kv_same, 1)
    last = lax.dynamic_index_in_dim(kv_same, head_at ^ (kv_heads - 1), 0, keepdims=False)
    reach = 2 * group - (share - 1)
    halo = routed(last[rows - HALO :, HEAD_SIZE:], reach, lambda i: i % share == share - 1)
    lanes = 2 * HEAD_SIZE
    group_rows = kv_heads * rows
    scale = 1.0 / math.sqrt(rows * count * lax.axis_size("rep"))
    *grad_q, send, keep_old, keep_own, tap_keep = launch(
        functools.partial(attend_kernel, scale, kv_heads),
        [shape((rows, own_width), bf16)] * kv_heads
        + [
            shape((2 * group_rows + HALO, lanes), bf16),
            shape((group_rows, lanes), f32),
            shape((group_rows, lanes), f32),
            shape((tap_count, HEAD_SIZE // 2), f32),
        ],
        (kv_same, kv_other, old_same, old_other, halo, conv_taps, *query_grads),
        scratch=[
            pltpu.VMEM((2 * WINDOW, HEAD_SIZE), bf16),
            pltpu.VMEM((HEAD_SIZE, 2 * WINDOW), bf16),
            pltpu.VMEM((HALO + 2 * WINDOW, HEAD_SIZE), f32),
            pltpu.VMEM((2 * WINDOW, HEAD_SIZE), bf16),
            pltpu.VMEM((2 * WINDOW, HEAD_SIZE), f32),
            pltpu.VMEM((HALO + 2 * WINDOW + HALO, HEAD_SIZE), f32),
        ]
        + [pltpu.VMEM((WINDOW, lanes), f32)] * 4
        + [pltpu.VMEM((WINDOW + rows, lanes), bf16)] * 4,
        flops=10 * kv_heads * rows * (WINDOW + rows) * own_width,
    )
    got = flipped(send, 1)
    note = got[2 * group_rows :].astype(f32)
    old_sum = (keep_old + got[:group_rows].astype(f32)).astype(bf16)
    grad_q = after([old_sum], *grad_q)
    returned = routed(old_sum, -group)
    grad_q = exchanged(grad_q)
    halo, tap_grads = note[:, HEAD_SIZE:], note[:, : HEAD_SIZE // 2]
    tap_grads = tap_keep + (tap_grads[:tap_count] + tap_grads[tap_count : 2 * tap_count])
    short = planes == tap_count == 4
    if short:
        low, high = jnp.split(tap_grads, 2)
        mine, theirs = jnp.where(plane < 2, low, high), jnp.where(plane < 2, high, low)
        theirs = jnp.pad(theirs, ((0, 6), (0, HEAD_SIZE // 2)))
        note = flipped(jnp.concatenate([halo, theirs], axis=0), 2 * group)
        tap_grads = mine + note[HALO : HALO + 2, : HEAD_SIZE // 2]
        returned_halo = jnp.where(plane < 2, note[:HALO], 0.0)
    else:
        returned_halo = routed(halo, -2 * group)
    (keep_own,) = after(grad_q, keep_own)
    total = keep_own + got[group_rows : 2 * group_rows].astype(f32) + returned.astype(f32)
    halo_block = jnp.pad(returned_halo, ((rows - HALO, 0), (HEAD_SIZE, 0)))
    owned = []
    for turn in range(kv_heads):
        mine = total[turn * rows : (turn + 1) * rows]
        owned.append((mine + jnp.where((head_at ^ turn) == kv_heads - 1, halo_block, 0.0)).astype(bf16))
    grad_q = after(owned, *grad_q)
    owned = exchanged(owned)
    (grad_queries,) = launch(unpack_queries_kernel, [shape((rows, width), bf16)], tuple(grad_q))
    owned = after([grad_queries], *owned)
    grad_keys, grad_values = launch(
        unpack_kernel, [shape((rows, kv_width), bf16), shape((rows, kv_width), bf16)], tuple(owned)
    )
    if short:
        low, high = tap_grads[0], tap_grads[1]
        even = plane % 2 == 0
        grad_taps = jnp.where(even, low, high) + flipped(jnp.where(even, high, low), group)
    else:
        spread = jnp.zeros((tap_count, kv_width), f32)
        spread = lax.dynamic_update_slice(spread, tap_grads, (0, (2 * head_at + parity) * (HEAD_SIZE // 2)))
        grad_taps = jnp.sum(lax.all_to_all(spread.reshape(count, -1), "seq", 0, 0, tiled=True), axis=0)
    grad_taps = lax.psum(grad_taps, "rep")
    return grad_queries[None], grad_keys[None], grad_values[None], grad_taps


def solution(mesh):
    in_specs = (
        P("rep", "seq", None),
        P("rep", "seq", None),
        P("rep", "seq", None),
        P(),
        P("rep", "seq", None),
    )
    out_specs = (P("rep", "seq", None), P("rep", "seq", None), P("rep", "seq", None), P("seq"))
    return jax.shard_map(
        on_device, mesh=mesh, in_specs=in_specs, out_specs=out_specs, check_vma=False
    )
```

```python
import functools
import math

import jax
import jax.numpy as jnp
from jax import lax
from jax.experimental import pallas as pl
from jax.experimental.pallas import tpu as pltpu
from jax.sharding import PartitionSpec as P

HEAD_SIZE = 128
WINDOW = 1024
NEG_FILL = -1e30
HALO = 16
VMEM_BYTES = 18 * 1024 * 1024
NT = (((1,), (1,)), ((), ()))


def place_of(group, share):
    device = lax.axis_index("seq")
    return lax.div(device, group), lax.rem(device, share), lax.div(lax.rem(device, group), share)


def run(kernel, out_shape, operands, scratch=(), flops=0, held=True, made=True):
    vmem = pl.BlockSpec(memory_space=pltpu.VMEM)
    home = pltpu.VMEM if held else pltpu.HBM
    moved = list(operands) + list(out_shape)
    operands = [pltpu.with_memory_space_constraint(a, home) for a in operands]
    return pl.pallas_call(
        kernel,
        out_shape=[pltpu.VMEM(a.shape, a.dtype) for a in out_shape] if made else out_shape,
        in_specs=[pl.BlockSpec(memory_space=home)] * len(operands),
        out_specs=[vmem] * len(out_shape),
        scratch_shapes=list(scratch),
        cost_estimate=pl.CostEstimate(
            flops=flops, bytes_accessed=sum(math.prod(a.shape) * a.dtype.itemsize for a in moved), transcendentals=0
        ),
        compiler_params=pltpu.CompilerParams(vmem_limit_bytes=VMEM_BYTES),
    )(*operands)


def columns_of(index, width=HEAD_SIZE):
    return pl.ds(pl.multiple_of(index * width, HEAD_SIZE), width)


def pack_kernel(place, queries, grad_out, keys, values, *refs):
    *parts, sems = refs
    rows = queries.shape[0]
    turns = len(parts) // 2
    heads = queries.shape[1] // HEAD_SIZE // turns
    moves = []
    for turn in range(turns):
        target = place[2] ^ turn
        moves.append((keys, target, parts[turn].at[:, :HEAD_SIZE]))
        moves.append((values, target, parts[turn].at[:, HEAD_SIZE:]))
    for turn in range(turns):
        target = place[2] ^ turn
        for base, source in ((0, queries), (heads, grad_out)):
            for head in range(heads):
                at = pl.ds((base + head) * rows, rows)
                moves.append((source, target * heads + head, parts[turns + turn].at[at]))
    copies = [
        pltpu.make_async_copy(source.at[:, columns_of(column)], target, sems.at[n])
        for n, (source, column, target) in enumerate(moves)
    ]
    for copy in copies:
        copy.start()
    for copy in copies:
        copy.wait()


def unpack_queries_kernel(place, *refs):
    parts, grad_queries = refs[:-1], refs[-1]
    for turn, part in enumerate(parts):
        grad_queries[:, columns_of(place[2] ^ turn, part.shape[1])] = part[...]


def attend_kernel(scale, turns, place, *refs):
    kv_same, kv_other, old_same, old_other, halo, all_taps = refs[:6]
    query_grads = refs[6 : 6 + turns]
    grad_qs = refs[6 + turns : 6 + 2 * turns]
    send, keep_old, keep_own, tap_keep = refs[6 + 2 * turns : 10 + 2 * turns]
    key_all, key_t, value_all, mix_all, dkey, dmix, *work = refs[10 + 2 * turns :]
    rows, width = grad_qs[0].shape
    blocks = turns
    span = 2 * blocks
    length = span * rows
    lanes = 2 * HEAD_SIZE
    pairs = width // lanes
    tap_count = all_taps.shape[0]
    group_at, parity, head_at = place
    taps = all_taps[:, columns_of(head_at)]
    inv_root = 1.0 / math.sqrt(HEAD_SIZE)
    log2_scale = inv_root * math.log2(math.e)
    score_refs, gprob_refs, low_refs, dscore_refs = work[0:2], work[2:4], work[4:6], work[6:8]

    def block_at(turn, core):
        return 2 * (head_at ^ turn) + core

    value_all[:HALO] = halo[...].astype(jnp.float32)
    for start, same, other in ((0, old_same, old_other), (span, kv_same, kv_other)):
        for turn in range(blocks):
            for source, core in ((same, parity), (other, 1 - parity)):
                first = pl.multiple_of((start + block_at(turn, core)) * rows, rows)
                key_all[pl.ds(first, rows)] = source[turn, :, :HEAD_SIZE]
                value_all[pl.ds(first + HALO, rows)] = source[turn, :, HEAD_SIZE:].astype(jnp.float32)
    for start in range(HALO, HALO + 2 * length, rows):
        mixed = taps[0:1] * value_all[start : start + rows]
        for index_k in range(1, tap_count):
            mixed = mixed + taps[index_k : index_k + 1] * value_all[start - index_k : start - index_k + rows]
        mix_all[start - HALO : start - HALO + rows] = mixed.astype(jnp.bfloat16)
    key_t[...] = jnp.transpose(key_all[...])
    dkey[...] = jnp.zeros_like(dkey)
    dmix[...] = jnp.zeros_like(dmix)
    fill = jnp.where(group_at == 0, NEG_FILL, 0.0).astype(jnp.float32)
    key_at = lax.broadcasted_iota(jnp.int32, (rows, lanes), 0)
    query_at = lax.broadcasted_iota(jnp.int32, (rows, lanes), 1) & (rows - 1)
    causal = key_at <= query_at
    stats = {}

    def places(n):
        step, pair = n // pairs, n % pairs
        number = block_at(step, parity)
        return step, pair, number, pl.multiple_of(number * rows, rows)

    def stacked(step, base):
        return query_grads[step][base // HEAD_SIZE * rows : (base + lanes) // HEAD_SIZE * rows]

    def by_eight(array):
        return array.reshape(-1, 8, array.shape[1])

    def scores_stage(n):
        step, pair, number, first = places(n)
        seen = pl.ds(first, length + rows)
        scores = lax.dot_general(
            key_all[seen], stacked(step, pair * lanes), NT, preferred_element_type=jnp.float32
        )
        grads = lax.dot_general(
            mix_all[seen], stacked(step, width + pair * lanes), NT, preferred_element_type=jnp.float32
        )
        edge = jnp.where(causal, scores[length:], scores[:rows] + fill)
        score_refs[n % 2][:rows] = edge
        score_refs[n % 2][rows:] = scores[rows:length]
        gprob_refs[n % 2][:rows] = jnp.where(causal, grads[length:], grads[:rows])
        gprob_refs[n % 2][rows:] = grads[rows:length]
        peak = jnp.max(by_eight(edge), axis=0)
        for c in range(1, span):
            part = jnp.max(by_eight(scores[c * rows : (c + 1) * rows]), axis=0)
            peak = jnp.maximum(peak, part + jnp.where(number + c < span, fill, 0.0))
        stats[n] = jnp.max(peak, axis=0, keepdims=True) * log2_scale

    def softmax_stage(n):
        step, pair, number, first = places(n)
        peak = stats[n]
        scores, gprob, low, dscore = (refs[n % 2] for refs in (score_refs, gprob_refs, low_refs, dscore_refs))
        total = jnp.zeros((8, lanes), jnp.float32)
        delta = jnp.zeros((8, lanes), jnp.float32)
        for c in range(span):
            at = slice(c * rows, (c + 1) * rows)
            shift = -peak if c == 0 else jnp.where(number + c < span, fill, 0.0) - peak
            prob = jnp.exp2(scores[at] * log2_scale + shift)
            total = total + jnp.sum(by_eight(prob), axis=0)
            delta = delta + jnp.sum(by_eight(prob * gprob[at]), axis=0)
            low[at] = prob.astype(jnp.bfloat16)
        inverse = 1.0 / jnp.sum(total, axis=0, keepdims=True)
        delta = jnp.sum(delta, axis=0, keepdims=True) * inverse
        for c in range(span):
            at = slice(c * rows, (c + 1) * rows)
            dscore[at] = low[at] * (gprob[at] - delta).astype(jnp.bfloat16)
        zero = jnp.zeros((), jnp.bfloat16)
        for ref in (low, dscore):
            edge = ref[:rows]
            ref[length:] = jnp.where(causal, edge, zero)
            ref[:rows] = jnp.where(causal, zero, edge)
        stats[n] = inverse

    def gradient_stage(n):
        step, pair, number, first = places(n)
        seen = pl.ds(first, length + rows)
        inverse = stats[n]
        column = jnp.transpose(jnp.broadcast_to(inverse, (HEAD_SIZE, lanes)))
        query = (stacked(step, pair * lanes).astype(jnp.float32) * column).astype(jnp.bfloat16)
        grad = (stacked(step, width + pair * lanes).astype(jnp.float32) * column).astype(jnp.bfloat16)
        low, dscore = low_refs[n % 2], dscore_refs[n % 2]
        dmix[pl.ds(first + HALO, length + rows)] += jnp.dot(low[...], grad, preferred_element_type=jnp.float32)
        dkey[seen] += jnp.dot(dscore[...], query, preferred_element_type=jnp.float32)
        dquery = jnp.dot(key_t[:, seen], dscore[...], preferred_element_type=jnp.float32)
        dquery = jnp.transpose(dquery * (inverse * inv_root)).astype(jnp.bfloat16)
        for h in range(2):
            base = pair * lanes + h * HEAD_SIZE
            grad_qs[step][:, base : base + HEAD_SIZE] = dquery[h * rows : (h + 1) * rows]

    count = blocks * pairs
    for n in range(count + 2):
        if n < count:
            scores_stage(n)
        if 1 <= n <= count:
            softmax_stage(n - 1)
        if n >= 2:
            gradient_stage(n - 2)

    def convolved(start, size):
        total = taps[0:1] * dmix[pl.ds(start, size)]
        for index_k in range(1, tap_count):
            total = total + taps[index_k : index_k + 1] * dmix[pl.ds(start + index_k, size)]
        return total

    for start, keep, base in ((0, keep_old, 0), (span, keep_own, blocks * rows)):
        for turn in range(blocks):
            for target, core, offset in ((keep, parity, 0), (send, 1 - parity, base)):
                first = pl.multiple_of((start + block_at(turn, core)) * rows, rows)
                at = slice(offset + turn * rows, offset + (turn + 1) * rows)
                target[at, :HEAD_SIZE] = (dkey[pl.ds(first, rows)] * inv_root).astype(target.dtype)
                target[at, HEAD_SIZE:] = convolved(first + HALO, rows).astype(target.dtype)
    note = slice(2 * blocks * rows, 2 * blocks * rows + HALO)
    send[note, HEAD_SIZE:] = convolved(0, HALO).astype(send.dtype)
    sums = [jnp.zeros((8, HEAD_SIZE), jnp.float32)] * tap_count
    for start in range(HALO, HALO + 2 * length, rows):
        grad = dmix[start : start + rows]
        for index_k in range(tap_count):
            sums[index_k] = sums[index_k] + jnp.sum(
                by_eight(grad * value_all[start - index_k : start - index_k + rows]), axis=0
            )
    tap_grads = jnp.concatenate([jnp.sum(total, axis=0, keepdims=True) for total in sums], axis=0) * scale
    low, high = tap_grads[:, : HEAD_SIZE // 2], tap_grads[:, HEAD_SIZE // 2 :]
    tap_keep[...] = jnp.where(parity == 0, low, high)
    theirs = jnp.where(parity == 0, high, low)
    upper = theirs.astype(send.dtype).astype(jnp.float32)
    theirs = jnp.concatenate([upper, theirs - upper], axis=0)
    theirs = jnp.concatenate([theirs, jnp.zeros((HALO - 2 * tap_count, HEAD_SIZE // 2), jnp.float32)], axis=0)
    theirs = jnp.concatenate([theirs, jnp.zeros_like(theirs)], axis=1)
    send[note, :HEAD_SIZE] = theirs.astype(send.dtype)


def on_device(queries, keys, values, conv_taps, grad_out):
    rows, width = queries.shape[1:]
    kv_width = keys.shape[2]
    tap_count = conv_taps.shape[0]
    kv_heads = kv_width // HEAD_SIZE
    group = WINDOW // rows
    share = group // kv_heads
    count = lax.axis_size("seq")
    planes = count // group
    own_width = width // kv_heads
    bf16, f32 = jnp.bfloat16, jnp.float32
    shape = jax.ShapeDtypeStruct
    plane, parity, head_at = place_of(group, share)

    def launch(kernel, out_shape, operands, **options):
        return run(lambda *refs: kernel(place_of(group, share), *refs), out_shape, operands, **options)

    def routed(array, distance, chosen=lambda i: True):
        route = [(i, i + distance) for i in range(count) if 0 <= i + distance < count and chosen(i)]
        return lax.ppermute(array, "seq", route)

    def flipped(array, bits):
        return lax.ppermute(array, "seq", [(i, i ^ bits) for i in range(count)])

    def after(others, *arrays):
        return lax.optimization_barrier((*arrays, *others))[: len(arrays)]

    def exchanged(parts):
        return [parts[0]] + [flipped(parts[turn], turn * share) for turn in range(1, kv_heads)]

    kv_shape = shape((rows, 2 * HEAD_SIZE), bf16)
    query_shape = shape((2 * own_width // HEAD_SIZE * rows, HEAD_SIZE), bf16)
    parts = launch(
        pack_kernel,
        [kv_shape] * kv_heads + [query_shape] * kv_heads,
        (queries[0], grad_out[0], keys[0], values[0]),
        scratch=[pltpu.SemaphoreType.DMA((2 * kv_heads * (1 + own_width // HEAD_SIZE),))],
        held=False,
    )
    kv_same = jnp.stack(exchanged(parts[:kv_heads]))
    old_same = routed(kv_same, group)
    query_grads = exchanged(after([kv_same], *parts[kv_heads:]))
    kv_same, old_same = lax.optimization_barrier((kv_same, old_same))
    old_other = flipped(old_same, 1)
    kv_other = flipped(kv_same, 1)
    last = lax.dynamic_index_in_dim(kv_same, head_at ^ (kv_heads - 1), 0, keepdims=False)
    reach = 2 * group - (share - 1)
    halo = routed(last[rows - HALO :, HEAD_SIZE:], reach, lambda i: i % share == share - 1)
    lanes = 2 * HEAD_SIZE
    group_rows = kv_heads * rows
    operands = (kv_same, kv_other, old_same, old_other, halo, conv_taps, *query_grads)
    results = [shape((rows, own_width), bf16)] * kv_heads + [
        shape((2 * group_rows + HALO, lanes), bf16),
        shape((group_rows, lanes), bf16),
        shape((group_rows, lanes), bf16),
        shape((tap_count, HEAD_SIZE // 2), f32),
    ]
    scale = 1.0 / math.sqrt(rows * count * lax.axis_size("rep"))
    *grad_q, send, keep_old, keep_own, tap_keep = launch(
        functools.partial(attend_kernel, scale, kv_heads),
        results,
        operands,
        scratch=[
            pltpu.VMEM((2 * WINDOW, HEAD_SIZE), bf16),
            pltpu.VMEM((HEAD_SIZE, 2 * WINDOW), bf16),
            pltpu.VMEM((HALO + 2 * WINDOW, HEAD_SIZE), f32),
            pltpu.VMEM((2 * WINDOW, HEAD_SIZE), bf16),
            pltpu.VMEM((2 * WINDOW, HEAD_SIZE), f32),
            pltpu.VMEM((HALO + 2 * WINDOW + HALO, HEAD_SIZE), f32),
        ]
        + [pltpu.VMEM((WINDOW, lanes), f32)] * 4
        + [pltpu.VMEM((WINDOW + rows, lanes), bf16)] * 4,
        flops=10 * kv_heads * rows * (WINDOW + rows) * own_width,
    )
    got = flipped(send, 1)
    note = got[2 * group_rows :].astype(f32)
    old_sum = (keep_old.astype(f32) + got[:group_rows].astype(f32)).astype(bf16)
    note, *grad_q = after([old_sum], note, *grad_q)
    returned = routed(old_sum, -group)
    grad_q = exchanged(grad_q)
    halo, tap_grads = note[:, HEAD_SIZE:], note[:, : HEAD_SIZE // 2]
    tap_grads = tap_keep + (tap_grads[:tap_count] + tap_grads[tap_count : 2 * tap_count])
    short = planes == tap_count == 4
    if short:
        low, high = jnp.split(tap_grads, 2)
        mine, theirs = jnp.where(plane < 2, low, high), jnp.where(plane < 2, high, low)
        theirs = jnp.pad(theirs, ((0, 6), (0, HEAD_SIZE // 2)))
        note = flipped(jnp.concatenate([halo, theirs], axis=0), 2 * group)
        tap_grads = mine + note[HALO : HALO + 2, : HEAD_SIZE // 2]
        returned_halo = jnp.where(plane < 2, note[:HALO], 0.0)
    else:
        returned_halo = routed(halo, -2 * group)
    (keep_own,) = after(grad_q, keep_own)
    total = keep_own.astype(f32) + got[group_rows : 2 * group_rows].astype(f32) + returned.astype(f32)
    halo_block = jnp.pad(returned_halo, ((rows - HALO, 0), (HEAD_SIZE, 0)))
    owned = []
    for turn in range(kv_heads):
        mine = total[turn * rows : (turn + 1) * rows]
        owned.append((mine + jnp.where((head_at ^ turn) == kv_heads - 1, halo_block, 0.0)).astype(bf16))
    grad_q = after(owned, *grad_q)
    owned = exchanged(owned)
    (grad_queries,) = launch(unpack_queries_kernel, [shape((rows, width), bf16)], tuple(grad_q), made=False)

    def in_order(parts):
        heads = []
        for head in range(kv_heads):
            chosen = parts[0]
            for turn in range(1, kv_heads):
                chosen = jnp.where((head_at ^ turn) == head, parts[turn], chosen)
            heads.append(chosen)
        return jnp.concatenate(heads, axis=1)

    grad_keys = in_order([part[:, :HEAD_SIZE] for part in owned])
    grad_values = in_order([part[:, HEAD_SIZE:] for part in owned])
    if short:
        low, high = tap_grads[0], tap_grads[1]
        even = plane % 2 == 0
        grad_taps = jnp.where(even, low, high) + flipped(jnp.where(even, high, low), group)
    else:
        spread = jnp.zeros((tap_count, kv_width), f32)
        spread = lax.dynamic_update_slice(spread, tap_grads, (0, (2 * head_at + parity) * (HEAD_SIZE // 2)))
        grad_taps = jnp.sum(lax.all_to_all(spread.reshape(count, -1), "seq", 0, 0, tiled=True), axis=0)
    grad_taps = lax.psum(grad_taps, "rep")
    return grad_queries[None], grad_keys[None], grad_values[None], grad_taps


def solution(mesh):
    in_specs = (
        P("rep", "seq", None),
        P("rep", "seq", None),
        P("rep", "seq", None),
        P(),
        P("rep", "seq", None),
    )
    out_specs = (P("rep", "seq", None), P("rep", "seq", None), P("rep", "seq", None), P("seq"))
    return jax.shard_map(
        on_device, mesh=mesh, in_specs=in_specs, out_specs=out_specs, check_vma=False
    )
```

```python
import functools
import math

import jax
import jax.numpy as jnp
from jax import lax
from jax.experimental import pallas as pl
from jax.experimental.pallas import tpu as pltpu
from jax.sharding import PartitionSpec as P

HEAD_SIZE = 128
WINDOW = 1024
NEG_FILL = -1e30
HALO = 16
VMEM_BYTES = 18 * 1024 * 1024
NT = (((1,), (1,)), ((), ()))


def place_of(group, share):
    device = lax.axis_index("seq")
    return lax.div(device, group), lax.rem(device, share), lax.div(lax.rem(device, group), share)


def run(kernel, out_shape, operands, scratch=(), flops=0, held=True, made=True):
    vmem = pl.BlockSpec(memory_space=pltpu.VMEM)
    home = pltpu.VMEM if held else pltpu.HBM
    moved = list(operands) + list(out_shape)
    operands = [pltpu.with_memory_space_constraint(a, home) for a in operands]
    return pl.pallas_call(
        kernel,
        out_shape=[pltpu.VMEM(a.shape, a.dtype) for a in out_shape] if made else out_shape,
        in_specs=[pl.BlockSpec(memory_space=home)] * len(operands),
        out_specs=[vmem] * len(out_shape),
        scratch_shapes=list(scratch),
        cost_estimate=pl.CostEstimate(
            flops=flops, bytes_accessed=sum(math.prod(a.shape) * a.dtype.itemsize for a in moved), transcendentals=0
        ),
        compiler_params=pltpu.CompilerParams(vmem_limit_bytes=VMEM_BYTES),
    )(*operands)


def columns_of(index, width=HEAD_SIZE):
    return pl.ds(pl.multiple_of(index * width, HEAD_SIZE), width)


def pack_kernel(place, queries, grad_out, keys, values, *refs):
    *parts, sems = refs
    rows = queries.shape[0]
    turns = len(parts) // 2
    heads = queries.shape[1] // HEAD_SIZE // turns
    moves = []
    for turn in range(turns):
        target = place[2] ^ turn
        moves.append((keys, target, parts[turn].at[:, :HEAD_SIZE]))
        moves.append((values, target, parts[turn].at[:, HEAD_SIZE:]))
    for turn in range(turns):
        target = place[2] ^ turn
        for base, source in ((0, queries), (heads, grad_out)):
            for head in range(heads):
                at = pl.ds((base + head) * rows, rows)
                moves.append((source, target * heads + head, parts[turns + turn].at[at]))
    copies = [
        pltpu.make_async_copy(source.at[:, columns_of(column)], target, sems.at[n])
        for n, (source, column, target) in enumerate(moves)
    ]
    for copy in copies:
        copy.start()
    for copy in copies:
        copy.wait()


def unpack_queries_kernel(place, *refs):
    parts, grad_queries = refs[:-1], refs[-1]
    for turn, part in enumerate(parts):
        grad_queries[:, columns_of(place[2] ^ turn, part.shape[1])] = part[...]


def attend_kernel(scale, turns, place, *refs):
    kv_same, kv_other, old_same, old_other, halo, all_taps = refs[:6]
    query_grads = refs[6 : 6 + turns]
    send, keep_old, keep_own, tap_keep = refs[6 + turns : 10 + turns]
    grad_qs = refs[10 + turns : 10 + 2 * turns]
    key_all, key_t, value_all, mix_all, dkey, dmix, *work = refs[10 + 2 * turns :]
    rows, width = grad_qs[0].shape
    blocks = turns
    span = 2 * blocks
    length = span * rows
    lanes = 2 * HEAD_SIZE
    pairs = width // lanes
    tap_count = all_taps.shape[0]
    group_at, parity, head_at = place
    taps = all_taps[:, columns_of(head_at)]
    inv_root = 1.0 / math.sqrt(HEAD_SIZE)
    log2_scale = inv_root * math.log2(math.e)
    score_refs, gprob_refs, low_refs, dscore_refs = work[0:2], work[2:4], work[4:6], work[6:8]

    def block_at(turn, core):
        return 2 * (head_at ^ turn) + core

    value_all[:HALO] = halo[...].astype(jnp.float32)
    for start, same, other in ((0, old_same, old_other), (span, kv_same, kv_other)):
        for turn in range(blocks):
            for source, core in ((same, parity), (other, 1 - parity)):
                first = pl.multiple_of((start + block_at(turn, core)) * rows, rows)
                key_all[pl.ds(first, rows)] = source[turn, :, :HEAD_SIZE]
                value_all[pl.ds(first + HALO, rows)] = source[turn, :, HEAD_SIZE:].astype(jnp.float32)
    for start in range(HALO, HALO + 2 * length, rows):
        mixed = taps[0:1] * value_all[start : start + rows]
        for index_k in range(1, tap_count):
            mixed = mixed + taps[index_k : index_k + 1] * value_all[start - index_k : start - index_k + rows]
        mix_all[start - HALO : start - HALO + rows] = mixed.astype(jnp.bfloat16)
    key_t[...] = jnp.transpose(key_all[...])
    dkey[...] = jnp.zeros_like(dkey)
    dmix[...] = jnp.zeros_like(dmix)
    fill = jnp.where(group_at == 0, NEG_FILL, 0.0).astype(jnp.float32)
    key_at = lax.broadcasted_iota(jnp.int32, (rows, lanes), 0)
    query_at = lax.broadcasted_iota(jnp.int32, (rows, lanes), 1) & (rows - 1)
    causal = key_at <= query_at
    stats = {}

    def places(n):
        step, pair = n // pairs, n % pairs
        number = block_at(step, parity)
        return step, pair, number, pl.multiple_of(number * rows, rows)

    def stacked(step, base):
        return query_grads[step][base // HEAD_SIZE * rows : (base + lanes) // HEAD_SIZE * rows]

    def by_eight(array):
        return array.reshape(-1, 8, array.shape[1])

    def scores_stage(n):
        step, pair, number, first = places(n)
        seen = pl.ds(first, length + rows)
        scores = lax.dot_general(
            key_all[seen], stacked(step, pair * lanes), NT, preferred_element_type=jnp.float32
        )
        grads = lax.dot_general(
            mix_all[seen], stacked(step, width + pair * lanes), NT, preferred_element_type=jnp.float32
        )
        edge = jnp.where(causal, scores[length:], scores[:rows] + fill)
        score_refs[n % 2][:rows] = edge
        score_refs[n % 2][rows:] = scores[rows:length]
        gprob_refs[n % 2][:rows] = jnp.where(causal, grads[length:], grads[:rows])
        gprob_refs[n % 2][rows:] = grads[rows:length]
        peak = jnp.max(by_eight(edge), axis=0)
        for c in range(1, span):
            part = jnp.max(by_eight(scores[c * rows : (c + 1) * rows]), axis=0)
            peak = jnp.maximum(peak, part + jnp.where(number + c < span, fill, 0.0))
        stats[n] = jnp.max(peak, axis=0, keepdims=True) * log2_scale

    def softmax_stage(n):
        step, pair, number, first = places(n)
        peak = stats[n]
        scores, gprob, low, dscore = (refs[n % 2] for refs in (score_refs, gprob_refs, low_refs, dscore_refs))
        total = jnp.zeros((8, lanes), jnp.float32)
        delta = jnp.zeros((8, lanes), jnp.float32)
        for c in range(span):
            at = slice(c * rows, (c + 1) * rows)
            shift = -peak if c == 0 else jnp.where(number + c < span, fill, 0.0) - peak
            prob = jnp.exp2(scores[at] * log2_scale + shift)
            total = total + jnp.sum(by_eight(prob), axis=0)
            delta = delta + jnp.sum(by_eight(prob * gprob[at]), axis=0)
            low[at] = prob.astype(jnp.bfloat16)
        inverse = 1.0 / jnp.sum(total, axis=0, keepdims=True)
        delta = jnp.sum(delta, axis=0, keepdims=True) * inverse
        for c in range(span):
            at = slice(c * rows, (c + 1) * rows)
            dscore[at] = low[at] * (gprob[at] - delta).astype(jnp.bfloat16)
        zero = jnp.zeros((), jnp.bfloat16)
        for ref in (low, dscore):
            edge = ref[:rows]
            ref[length:] = jnp.where(causal, edge, zero)
            ref[:rows] = jnp.where(causal, zero, edge)
        stats[n] = inverse

    def gradient_stage(n):
        step, pair, number, first = places(n)
        seen = pl.ds(first, length + rows)
        inverse = stats[n]
        column = jnp.transpose(jnp.broadcast_to(inverse, (HEAD_SIZE, lanes)))
        query = (stacked(step, pair * lanes).astype(jnp.float32) * column).astype(jnp.bfloat16)
        grad = (stacked(step, width + pair * lanes).astype(jnp.float32) * column).astype(jnp.bfloat16)
        low, dscore = low_refs[n % 2], dscore_refs[n % 2]
        dmix[pl.ds(first + HALO, length + rows)] += jnp.dot(low[...], grad, preferred_element_type=jnp.float32)
        dkey[seen] += jnp.dot(dscore[...], query, preferred_element_type=jnp.float32)
        dquery = jnp.dot(key_t[:, seen], dscore[...], preferred_element_type=jnp.float32)
        dquery = jnp.transpose(dquery * (inverse * inv_root)).astype(jnp.bfloat16)
        for h in range(2):
            base = pair * lanes + h * HEAD_SIZE
            grad_qs[step][:, base : base + HEAD_SIZE] = dquery[h * rows : (h + 1) * rows]

    count = blocks * pairs
    for n in range(count + 2):
        if n < count:
            scores_stage(n)
        if 1 <= n <= count:
            softmax_stage(n - 1)
        if n >= 2:
            gradient_stage(n - 2)

    def convolved(start, size):
        total = taps[0:1] * dmix[pl.ds(start, size)]
        for index_k in range(1, tap_count):
            total = total + taps[index_k : index_k + 1] * dmix[pl.ds(start + index_k, size)]
        return total

    for start, keep, base in ((0, keep_old, 0), (span, keep_own, blocks * rows)):
        for turn in range(blocks):
            for target, core, offset in ((keep, parity, 0), (send, 1 - parity, base)):
                first = pl.multiple_of((start + block_at(turn, core)) * rows, rows)
                at = slice(offset + turn * rows, offset + (turn + 1) * rows)
                target[at, :HEAD_SIZE] = (dkey[pl.ds(first, rows)] * inv_root).astype(target.dtype)
                target[at, HEAD_SIZE:] = convolved(first + HALO, rows).astype(target.dtype)
    note = slice(2 * blocks * rows, 2 * blocks * rows + HALO)
    send[note, HEAD_SIZE:] = convolved(0, HALO).astype(send.dtype)
    sums = [jnp.zeros((8, HEAD_SIZE), jnp.float32)] * tap_count
    for start in range(HALO, HALO + 2 * length, rows):
        grad = dmix[start : start + rows]
        for index_k in range(tap_count):
            sums[index_k] = sums[index_k] + jnp.sum(
                by_eight(grad * value_all[start - index_k : start - index_k + rows]), axis=0
            )
    tap_grads = jnp.concatenate([jnp.sum(total, axis=0, keepdims=True) for total in sums], axis=0) * scale
    low, high = tap_grads[:, : HEAD_SIZE // 2], tap_grads[:, HEAD_SIZE // 2 :]
    tap_keep[...] = jnp.where(parity == 0, low, high)
    theirs = jnp.where(parity == 0, high, low)
    upper = theirs.astype(send.dtype).astype(jnp.float32)
    theirs = jnp.concatenate([upper, theirs - upper], axis=0)
    theirs = jnp.concatenate([theirs, jnp.zeros((HALO - 2 * tap_count, HEAD_SIZE // 2), jnp.float32)], axis=0)
    theirs = jnp.concatenate([theirs, jnp.zeros_like(theirs)], axis=1)
    send[note, :HEAD_SIZE] = theirs.astype(send.dtype)


def on_device(queries, keys, values, conv_taps, grad_out):
    rows, width = queries.shape[1:]
    kv_width = keys.shape[2]
    tap_count = conv_taps.shape[0]
    kv_heads = kv_width // HEAD_SIZE
    group = WINDOW // rows
    share = group // kv_heads
    count = lax.axis_size("seq")
    planes = count // group
    own_width = width // kv_heads
    bf16, f32 = jnp.bfloat16, jnp.float32
    shape = jax.ShapeDtypeStruct
    plane, parity, head_at = place_of(group, share)

    def launch(kernel, out_shape, operands, **options):
        return run(lambda *refs: kernel(place_of(group, share), *refs), out_shape, operands, **options)

    def routed(array, distance, chosen=lambda i: True):
        route = [(i, i + distance) for i in range(count) if 0 <= i + distance < count and chosen(i)]
        return lax.ppermute(array, "seq", route)

    def flipped(array, bits):
        return lax.ppermute(array, "seq", [(i, i ^ bits) for i in range(count)])

    def after(others, *arrays):
        return lax.optimization_barrier((*arrays, *others))[: len(arrays)]

    def exchanged(parts):
        return [parts[0]] + [flipped(parts[turn], turn * share) for turn in range(1, kv_heads)]

    kv_shape = shape((rows, 2 * HEAD_SIZE), bf16)
    query_shape = shape((2 * own_width // HEAD_SIZE * rows, HEAD_SIZE), bf16)
    parts = launch(
        pack_kernel,
        [kv_shape] * kv_heads + [query_shape] * kv_heads,
        (queries[0], grad_out[0], keys[0], values[0]),
        scratch=[pltpu.SemaphoreType.DMA((2 * kv_heads * (1 + own_width // HEAD_SIZE),))],
        held=False,
    )
    kv_same = jnp.stack(exchanged(parts[:kv_heads]))
    old_same = routed(kv_same, group)
    query_grads = exchanged(after([kv_same], *parts[kv_heads:]))
    kv_same, old_same = lax.optimization_barrier((kv_same, old_same))
    old_other = flipped(old_same, 1)
    kv_other = flipped(kv_same, 1)
    last = lax.dynamic_index_in_dim(kv_same, head_at ^ (kv_heads - 1), 0, keepdims=False)
    reach = 2 * group - (share - 1)
    halo = routed(last[rows - HALO :, HEAD_SIZE:], reach, lambda i: i % share == share - 1)
    lanes = 2 * HEAD_SIZE
    group_rows = kv_heads * rows
    operands = (kv_same, kv_other, old_same, old_other, halo, conv_taps, *query_grads)
    results = [
        shape((2 * group_rows + HALO, lanes), bf16),
        shape((group_rows, lanes), bf16),
        shape((group_rows, lanes), bf16),
        shape((tap_count, HEAD_SIZE // 2), f32),
    ] + [shape((rows, own_width), bf16)] * kv_heads
    scale = 1.0 / math.sqrt(rows * count * lax.axis_size("rep"))
    send, keep_old, keep_own, tap_keep, *grad_q = launch(
        functools.partial(attend_kernel, scale, kv_heads),
        results,
        operands,
        scratch=[
            pltpu.VMEM((2 * WINDOW, HEAD_SIZE), bf16),
            pltpu.VMEM((HEAD_SIZE, 2 * WINDOW), bf16),
            pltpu.VMEM((HALO + 2 * WINDOW, HEAD_SIZE), f32),
            pltpu.VMEM((2 * WINDOW, HEAD_SIZE), bf16),
            pltpu.VMEM((2 * WINDOW, HEAD_SIZE), f32),
            pltpu.VMEM((HALO + 2 * WINDOW + HALO, HEAD_SIZE), f32),
        ]
        + [pltpu.VMEM((WINDOW, lanes), f32)] * 4
        + [pltpu.VMEM((WINDOW + rows, lanes), bf16)] * 4,
        flops=10 * kv_heads * rows * (WINDOW + rows) * own_width,
    )
    got = flipped(send, 1)
    note = got[2 * group_rows :].astype(f32)
    old_sum = (keep_old.astype(f32) + got[:group_rows].astype(f32)).astype(bf16)
    note, *grad_q = after([old_sum], note, *grad_q)
    returned = routed(old_sum, -group)
    grad_q = exchanged(grad_q)
    halo, tap_grads = note[:, HEAD_SIZE:], note[:, : HEAD_SIZE // 2]
    tap_grads = tap_keep + (tap_grads[:tap_count] + tap_grads[tap_count : 2 * tap_count])
    short = planes == tap_count == 4
    if short:
        low, high = jnp.split(tap_grads, 2)
        mine, theirs = jnp.where(plane < 2, low, high), jnp.where(plane < 2, high, low)
        theirs = jnp.pad(theirs, ((0, 6), (0, HEAD_SIZE // 2)))
        note = flipped(jnp.concatenate([halo, theirs], axis=0), 2 * group)
        tap_grads = mine + note[HALO : HALO + 2, : HEAD_SIZE // 2]
        returned_halo = jnp.where(plane < 2, note[:HALO], 0.0)
    else:
        returned_halo = routed(halo, -2 * group)
    total = keep_own.astype(f32) + got[group_rows : 2 * group_rows].astype(f32) + returned.astype(f32)
    halo_block = jnp.pad(returned_halo, ((rows - HALO, 0), (HEAD_SIZE, 0)))
    owned = []
    for turn in range(kv_heads):
        mine = total[turn * rows : (turn + 1) * rows]
        owned.append((mine + jnp.where((head_at ^ turn) == kv_heads - 1, halo_block, 0.0)).astype(bf16))
    grad_q = after(owned, *grad_q)
    owned = exchanged(owned)
    (grad_queries,) = launch(unpack_queries_kernel, [shape((rows, width), bf16)], tuple(grad_q), made=False)

    def in_order(parts):
        heads = []
        for head in range(kv_heads):
            chosen = parts[0]
            for turn in range(1, kv_heads):
                chosen = jnp.where((head_at ^ turn) == head, parts[turn], chosen)
            heads.append(chosen)
        return jnp.concatenate(heads, axis=1)

    grad_keys = in_order([part[:, :HEAD_SIZE] for part in owned])
    grad_values = in_order([part[:, HEAD_SIZE:] for part in owned])
    if short:
        low, high = tap_grads[0], tap_grads[1]
        even = plane % 2 == 0
        grad_taps = jnp.where(even, low, high) + flipped(jnp.where(even, high, low), group)
    else:
        spread = jnp.zeros((tap_count, kv_width), f32)
        spread = lax.dynamic_update_slice(spread, tap_grads, (0, (2 * head_at + parity) * (HEAD_SIZE // 2)))
        grad_taps = jnp.sum(lax.all_to_all(spread.reshape(count, -1), "seq", 0, 0, tiled=True), axis=0)
    grad_taps = lax.psum(grad_taps, "rep")
    return grad_queries[None], grad_keys[None], grad_values[None], grad_taps


def solution(mesh):
    in_specs = (
        P("rep", "seq", None),
        P("rep", "seq", None),
        P("rep", "seq", None),
        P(),
        P("rep", "seq", None),
    )
    out_specs = (P("rep", "seq", None), P("rep", "seq", None), P("rep", "seq", None), P("seq"))
    return jax.shard_map(
        on_device, mesh=mesh, in_specs=in_specs, out_specs=out_specs, check_vma=False
    )
```

```python
import functools
import math

import jax
import jax.numpy as jnp
from jax import lax
from jax.experimental import pallas as pl
from jax.experimental.pallas import tpu as pltpu
from jax.sharding import PartitionSpec as P

HEAD_SIZE = 128
WINDOW = 1024
NEG_FILL = -1e30
HALO = 16
VMEM_BYTES = 18 * 1024 * 1024
NT = (((1,), (1,)), ((), ()))


def place_of(group, share):
    device = lax.axis_index("seq")
    return lax.div(device, group), lax.rem(device, share), lax.div(lax.rem(device, group), share)


def run(kernel, out_shape, operands, scratch=(), flops=0, held=True, made=True):
    vmem = pl.BlockSpec(memory_space=pltpu.VMEM)
    home = pltpu.VMEM if held else pltpu.HBM
    moved = list(operands) + list(out_shape)
    operands = [pltpu.with_memory_space_constraint(a, home) for a in operands]
    return pl.pallas_call(
        kernel,
        out_shape=[pltpu.VMEM(a.shape, a.dtype) for a in out_shape] if made else out_shape,
        in_specs=[pl.BlockSpec(memory_space=home)] * len(operands),
        out_specs=[vmem] * len(out_shape),
        scratch_shapes=list(scratch),
        cost_estimate=pl.CostEstimate(
            flops=flops, bytes_accessed=sum(math.prod(a.shape) * a.dtype.itemsize for a in moved), transcendentals=0
        ),
        compiler_params=pltpu.CompilerParams(vmem_limit_bytes=VMEM_BYTES),
    )(*operands)


def columns_of(index, width=HEAD_SIZE):
    return pl.ds(pl.multiple_of(index * width, HEAD_SIZE), width)


def pack_kernel(place, queries, grad_out, keys, values, *refs):
    *parts, sems = refs
    rows = queries.shape[0]
    turns = len(parts) // 2
    heads = queries.shape[1] // HEAD_SIZE // turns
    moves = []
    for turn in range(turns):
        target = place[2] ^ turn
        moves.append((keys, target, parts[turn].at[:, :HEAD_SIZE]))
        moves.append((values, target, parts[turn].at[:, HEAD_SIZE:]))
    for turn in range(turns):
        target = place[2] ^ turn
        for base, source in ((0, queries), (heads, grad_out)):
            for head in range(heads):
                at = pl.ds((base + head) * rows, rows)
                moves.append((source, target * heads + head, parts[turns + turn].at[at]))
    copies = [
        pltpu.make_async_copy(source.at[:, columns_of(column)], target, sems.at[n])
        for n, (source, column, target) in enumerate(moves)
    ]
    for copy in copies:
        copy.start()
    for copy in copies:
        copy.wait()


def unpack_queries_kernel(place, *refs):
    parts, grad_queries = refs[:-1], refs[-1]
    for turn, part in enumerate(parts):
        grad_queries[:, columns_of(place[2] ^ turn, part.shape[1])] = part[...]


def by_eight(array):
    return array.reshape(-1, 8, array.shape[1])


def sweep(place, turns, query_grads, grad_qs, key_all, key_t, mix_all, dkey, dmix, work):
    rows, width = grad_qs[0].shape
    length = WINDOW
    span = length // rows
    lanes = 2 * HEAD_SIZE
    pairs = width // lanes
    group_at, parity, head_at = place
    inv_root = 1.0 / math.sqrt(HEAD_SIZE)
    log2_scale = inv_root * math.log2(math.e)
    score_refs, gprob_refs, low_refs, dscore_refs = work[0:2], work[2:4], work[4:6], work[6:8]
    fill = jnp.where(group_at == 0, NEG_FILL, 0.0).astype(jnp.float32)
    key_at = lax.broadcasted_iota(jnp.int32, (rows, lanes), 0)
    query_at = lax.broadcasted_iota(jnp.int32, (rows, lanes), 1) & (rows - 1)
    causal = key_at <= query_at
    stats = {}

    def places(n):
        step, pair = n // pairs, n % pairs
        number = block_at(place, turns[step], parity)
        return step, pair, number, pl.multiple_of(number * rows, rows)

    def stacked(step, base):
        return query_grads[step][base // HEAD_SIZE * rows : (base + lanes) // HEAD_SIZE * rows]

    def scores_stage(n):
        step, pair, number, first = places(n)
        seen = pl.ds(first, length + rows)
        scores = lax.dot_general(
            key_all[seen], stacked(step, pair * lanes), NT, preferred_element_type=jnp.float32
        )
        grads = lax.dot_general(
            mix_all[seen], stacked(step, width + pair * lanes), NT, preferred_element_type=jnp.float32
        )
        edge = jnp.where(causal, scores[length:], scores[:rows] + fill)
        score_refs[n % 2][:rows] = edge
        score_refs[n % 2][rows:] = scores[rows:length]
        gprob_refs[n % 2][:rows] = jnp.where(causal, grads[length:], grads[:rows])
        gprob_refs[n % 2][rows:] = grads[rows:length]
        peak = jnp.max(by_eight(edge), axis=0)
        for c in range(1, span):
            part = jnp.max(by_eight(scores[c * rows : (c + 1) * rows]), axis=0)
            peak = jnp.maximum(peak, part + jnp.where(number + c < span, fill, 0.0))
        stats[n] = jnp.max(peak, axis=0, keepdims=True) * log2_scale

    def softmax_stage(n):
        step, pair, number, first = places(n)
        peak = stats[n]
        scores, gprob, low, dscore = (refs[n % 2] for refs in (score_refs, gprob_refs, low_refs, dscore_refs))
        total = jnp.zeros((8, lanes), jnp.float32)
        delta = jnp.zeros((8, lanes), jnp.float32)
        for c in range(span):
            at = slice(c * rows, (c + 1) * rows)
            shift = -peak if c == 0 else jnp.where(number + c < span, fill, 0.0) - peak
            prob = jnp.exp2(scores[at] * log2_scale + shift)
            total = total + jnp.sum(by_eight(prob), axis=0)
            delta = delta + jnp.sum(by_eight(prob * gprob[at]), axis=0)
            low[at] = prob.astype(jnp.bfloat16)
        inverse = 1.0 / jnp.sum(total, axis=0, keepdims=True)
        delta = jnp.sum(delta, axis=0, keepdims=True) * inverse
        for c in range(span):
            at = slice(c * rows, (c + 1) * rows)
            dscore[at] = low[at] * (gprob[at] - delta).astype(jnp.bfloat16)
        zero = jnp.zeros((), jnp.bfloat16)
        for ref in (low, dscore):
            edge = ref[:rows]
            ref[length:] = jnp.where(causal, edge, zero)
            ref[:rows] = jnp.where(causal, zero, edge)
        stats[n] = inverse

    def gradient_stage(n):
        step, pair, number, first = places(n)
        seen = pl.ds(first, length + rows)
        inverse = stats[n]
        column = jnp.transpose(jnp.broadcast_to(inverse, (HEAD_SIZE, lanes)))
        query = (stacked(step, pair * lanes).astype(jnp.float32) * column).astype(jnp.bfloat16)
        grad = (stacked(step, width + pair * lanes).astype(jnp.float32) * column).astype(jnp.bfloat16)
        low, dscore = low_refs[n % 2], dscore_refs[n % 2]
        dmix[pl.ds(first + HALO, length + rows)] += jnp.dot(low[...], grad, preferred_element_type=jnp.float32)
        dkey[seen] += jnp.dot(dscore[...], query, preferred_element_type=jnp.float32)
        dquery = jnp.dot(key_t[:, seen], dscore[...], preferred_element_type=jnp.float32)
        dquery = jnp.transpose(dquery * (inverse * inv_root)).astype(jnp.bfloat16)
        for h in range(2):
            base = pair * lanes + h * HEAD_SIZE
            grad_qs[step][:, base : base + HEAD_SIZE] = dquery[h * rows : (h + 1) * rows]

    count = len(turns) * pairs
    for n in range(count + 2):
        if n < count:
            scores_stage(n)
        if 1 <= n <= count:
            softmax_stage(n - 1)
        if n >= 2:
            gradient_stage(n - 2)


def block_at(place, turn, core):
    return 2 * (place[2] ^ turn) + core


def attend_first_kernel(turns, place, *refs):
    kv_same, kv_other, old_same, old_other, halo, all_taps = refs[:6]
    query_grads, refs = refs[6 : 6 + turns], refs[6 + turns :]
    grad_qs, refs = refs[:turns], refs[turns:]
    key_all, key_t, mix_all, value_all, dkey, dmix, *work = refs
    blocks, rows = kv_same.shape[:2]
    span = 2 * blocks
    length = span * rows
    tap_count = all_taps.shape[0]
    parity = place[1]
    taps = all_taps[:, columns_of(place[2])]
    value_all[:HALO] = halo[...].astype(jnp.float32)
    for start, same, other in ((0, old_same, old_other), (span, kv_same, kv_other)):
        for turn in range(blocks):
            for source, core in ((same, parity), (other, 1 - parity)):
                first = pl.multiple_of((start + block_at(place, turn, core)) * rows, rows)
                key_all[pl.ds(first, rows)] = source[turn, :, :HEAD_SIZE]
                value_all[pl.ds(first + HALO, rows)] = source[turn, :, HEAD_SIZE:].astype(jnp.float32)
    for start in range(HALO, HALO + 2 * length, rows):
        mixed = taps[0:1] * value_all[start : start + rows]
        for index_k in range(1, tap_count):
            mixed = mixed + taps[index_k : index_k + 1] * value_all[start - index_k : start - index_k + rows]
        mix_all[start - HALO : start - HALO + rows] = mixed.astype(jnp.bfloat16)
    key_t[...] = jnp.transpose(key_all[...])
    dkey[...] = jnp.zeros_like(dkey)
    dmix[...] = jnp.zeros_like(dmix)
    sweep(place, range(turns), query_grads, grad_qs, key_all, key_t, mix_all, dkey, dmix, work)


def attend_last_kernel(scale, turns, place, *refs):
    all_taps, key_all, key_t, mix_all, value_all, dkey_before, dmix_before = refs[:7]
    query_grads, refs = refs[7 : 7 + turns], refs[7 + turns :]
    grad_qs, refs = refs[:turns], refs[turns:]
    send, keep_old, keep_own, tap_keep, dkey, dmix, *work = refs
    rows = grad_qs[0].shape[0]
    blocks = keep_old.shape[0] // rows
    span = 2 * blocks
    length = span * rows
    tap_count = all_taps.shape[0]
    parity = place[1]
    taps = all_taps[:, columns_of(place[2])]
    inv_root = 1.0 / math.sqrt(HEAD_SIZE)
    dkey[...] = dkey_before[...]
    dmix[...] = dmix_before[...]
    sweep(place, range(blocks - turns, blocks), query_grads, grad_qs, key_all, key_t, mix_all, dkey, dmix, work)

    def convolved(start, size):
        total = taps[0:1] * dmix[pl.ds(start, size)]
        for index_k in range(1, tap_count):
            total = total + taps[index_k : index_k + 1] * dmix[pl.ds(start + index_k, size)]
        return total

    for start, keep, base in ((0, keep_old, 0), (span, keep_own, blocks * rows)):
        for turn in range(blocks):
            for target, core, offset in ((keep, parity, 0), (send, 1 - parity, base)):
                first = pl.multiple_of((start + block_at(place, turn, core)) * rows, rows)
                at = slice(offset + turn * rows, offset + (turn + 1) * rows)
                target[at, :HEAD_SIZE] = (dkey[pl.ds(first, rows)] * inv_root).astype(target.dtype)
                target[at, HEAD_SIZE:] = convolved(first + HALO, rows).astype(target.dtype)
    note = slice(2 * blocks * rows, 2 * blocks * rows + HALO)
    send[note, HEAD_SIZE:] = convolved(0, HALO).astype(send.dtype)
    sums = [jnp.zeros((8, HEAD_SIZE), jnp.float32)] * tap_count
    for start in range(HALO, HALO + 2 * length, rows):
        grad = dmix[start : start + rows]
        for index_k in range(tap_count):
            sums[index_k] = sums[index_k] + jnp.sum(
                by_eight(grad * value_all[start - index_k : start - index_k + rows]), axis=0
            )
    tap_grads = jnp.concatenate([jnp.sum(total, axis=0, keepdims=True) for total in sums], axis=0) * scale
    low, high = tap_grads[:, : HEAD_SIZE // 2], tap_grads[:, HEAD_SIZE // 2 :]
    tap_keep[...] = jnp.where(parity == 0, low, high)
    theirs = jnp.where(parity == 0, high, low)
    upper = theirs.astype(send.dtype).astype(jnp.float32)
    theirs = jnp.concatenate([upper, theirs - upper], axis=0)
    theirs = jnp.concatenate([theirs, jnp.zeros((HALO - 2 * tap_count, HEAD_SIZE // 2), jnp.float32)], axis=0)
    theirs = jnp.concatenate([theirs, jnp.zeros_like(theirs)], axis=1)
    send[note, :HEAD_SIZE] = theirs.astype(send.dtype)


def on_device(queries, keys, values, conv_taps, grad_out):
    rows, width = queries.shape[1:]
    kv_width = keys.shape[2]
    tap_count = conv_taps.shape[0]
    kv_heads = kv_width // HEAD_SIZE
    group = WINDOW // rows
    share = group // kv_heads
    count = lax.axis_size("seq")
    planes = count // group
    own_width = width // kv_heads
    bf16, f32 = jnp.bfloat16, jnp.float32
    shape = jax.ShapeDtypeStruct
    plane, parity, head_at = place_of(group, share)

    def launch(kernel, out_shape, operands, **options):
        return run(lambda *refs: kernel(place_of(group, share), *refs), out_shape, operands, **options)

    def routed(array, distance, chosen=lambda i: True):
        route = [(i, i + distance) for i in range(count) if 0 <= i + distance < count and chosen(i)]
        return lax.ppermute(array, "seq", route)

    def flipped(array, bits):
        return lax.ppermute(array, "seq", [(i, i ^ bits) for i in range(count)])

    def after(others, *arrays):
        return lax.optimization_barrier((*arrays, *others))[: len(arrays)]

    def exchanged(parts):
        return [parts[0]] + [flipped(parts[turn], turn * share) for turn in range(1, kv_heads)]

    kv_shape = shape((rows, 2 * HEAD_SIZE), bf16)
    query_shape = shape((2 * own_width // HEAD_SIZE * rows, HEAD_SIZE), bf16)
    parts = launch(
        pack_kernel,
        [kv_shape] * kv_heads + [query_shape] * kv_heads,
        (queries[0], grad_out[0], keys[0], values[0]),
        scratch=[pltpu.SemaphoreType.DMA((2 * kv_heads * (1 + own_width // HEAD_SIZE),))],
        held=False,
    )
    kv_same = jnp.stack(exchanged(parts[:kv_heads]))
    old_same = routed(kv_same, group)
    query_grads = exchanged(after([kv_same], *parts[kv_heads:]))
    kv_same, old_same = lax.optimization_barrier((kv_same, old_same))
    old_other = flipped(old_same, 1)
    kv_other = flipped(kv_same, 1)
    last = lax.dynamic_index_in_dim(kv_same, head_at ^ (kv_heads - 1), 0, keepdims=False)
    reach = 2 * group - (share - 1)
    halo = routed(last[rows - HALO :, HEAD_SIZE:], reach, lambda i: i % share == share - 1)
    lanes = 2 * HEAD_SIZE
    group_rows = kv_heads * rows
    half = kv_heads - 1
    work = [pltpu.VMEM((WINDOW, lanes), f32)] * 4 + [pltpu.VMEM((WINDOW + rows, lanes), bf16)] * 4
    sums = [shape((2 * WINDOW, HEAD_SIZE), f32), shape((HALO + 2 * WINDOW + HALO, HEAD_SIZE), f32)]
    kept = [
        shape((2 * WINDOW, HEAD_SIZE), bf16),
        shape((HEAD_SIZE, 2 * WINDOW), bf16),
        shape((2 * WINDOW, HEAD_SIZE), bf16),
        shape((HALO + 2 * WINDOW, HEAD_SIZE), f32),
    ]
    *early, key_all, key_t, mix_all, value_all, dkey, dmix = launch(
        functools.partial(attend_first_kernel, half),
        [shape((rows, own_width), bf16)] * half + kept + sums,
        (kv_same, kv_other, old_same, old_other, halo, conv_taps, *query_grads[:half]),
        scratch=work,
    )
    scale = 1.0 / math.sqrt(rows * count * lax.axis_size("rep"))
    *late, send, keep_old, keep_own, tap_keep = launch(
        functools.partial(attend_last_kernel, scale, kv_heads - half),
        [shape((rows, own_width), bf16)] * (kv_heads - half)
        + [
            shape((2 * group_rows + HALO, lanes), bf16),
            shape((group_rows, lanes), bf16),
            shape((group_rows, lanes), bf16),
            shape((tap_count, HEAD_SIZE // 2), f32),
        ],
        (conv_taps, key_all, key_t, mix_all, value_all, dkey, dmix, *query_grads[half:]),
        scratch=[pltpu.VMEM(a.shape, a.dtype) for a in sums] + work,
    )
    got = flipped(send, 1)
    note = got[2 * group_rows :].astype(f32)
    old_sum = (keep_old.astype(f32) + got[:group_rows].astype(f32)).astype(bf16)
    note, *late = after([old_sum], note, *late)
    returned = routed(old_sum, -group)
    grad_q = exchanged([*early, *late])
    halo, tap_grads = note[:, HEAD_SIZE:], note[:, : HEAD_SIZE // 2]
    tap_grads = tap_keep + (tap_grads[:tap_count] + tap_grads[tap_count : 2 * tap_count])
    short = planes == tap_count == 4
    if short:
        low, high = jnp.split(tap_grads, 2)
        mine, theirs = jnp.where(plane < 2, low, high), jnp.where(plane < 2, high, low)
        theirs = jnp.pad(theirs, ((0, 6), (0, HEAD_SIZE // 2)))
        note = flipped(jnp.concatenate([halo, theirs], axis=0), 2 * group)
        tap_grads = mine + note[HALO : HALO + 2, : HEAD_SIZE // 2]
        returned_halo = jnp.where(plane < 2, note[:HALO], 0.0)
    else:
        returned_halo = routed(halo, -2 * group)
    total = keep_own.astype(f32) + got[group_rows : 2 * group_rows].astype(f32) + returned.astype(f32)
    halo_block = jnp.pad(returned_halo, ((rows - HALO, 0), (HEAD_SIZE, 0)))
    owned = []
    for turn in range(kv_heads):
        mine = total[turn * rows : (turn + 1) * rows]
        owned.append((mine + jnp.where((head_at ^ turn) == kv_heads - 1, halo_block, 0.0)).astype(bf16))
    grad_q = after(owned, *grad_q)
    owned = exchanged(owned)
    (grad_queries,) = launch(unpack_queries_kernel, [shape((rows, width), bf16)], tuple(grad_q), made=False)

    def in_order(parts):
        heads = []
        for head in range(kv_heads):
            chosen = parts[0]
            for turn in range(1, kv_heads):
                chosen = jnp.where((head_at ^ turn) == head, parts[turn], chosen)
            heads.append(chosen)
        return jnp.concatenate(heads, axis=1)

    grad_keys = in_order([part[:, :HEAD_SIZE] for part in owned])
    grad_values = in_order([part[:, HEAD_SIZE:] for part in owned])
    if short:
        low, high = tap_grads[0], tap_grads[1]
        even = plane % 2 == 0
        grad_taps = jnp.where(even, low, high) + flipped(jnp.where(even, high, low), group)
    else:
        spread = jnp.zeros((tap_count, kv_width), f32)
        spread = lax.dynamic_update_slice(spread, tap_grads, (0, (2 * head_at + parity) * (HEAD_SIZE // 2)))
        grad_taps = jnp.sum(lax.all_to_all(spread.reshape(count, -1), "seq", 0, 0, tiled=True), axis=0)
    grad_taps = lax.psum(grad_taps, "rep")
    return grad_queries[None], grad_keys[None], grad_values[None], grad_taps


def solution(mesh):
    in_specs = (
        P("rep", "seq", None),
        P("rep", "seq", None),
        P("rep", "seq", None),
        P(),
        P("rep", "seq", None),
    )
    out_specs = (P("rep", "seq", None), P("rep", "seq", None), P("rep", "seq", None), P("seq"))
    return jax.shard_map(
        on_device, mesh=mesh, in_specs=in_specs, out_specs=out_specs, check_vma=False
    )
```

```python
import functools
import math

import jax
import jax.numpy as jnp
from jax import lax
from jax.experimental import pallas as pl
from jax.experimental.pallas import tpu as pltpu
from jax.sharding import PartitionSpec as P

HEAD_SIZE = 128
WINDOW = 1024
NEG_FILL = -1e30
HALO = 16
VMEM_BYTES = 18 * 1024 * 1024
NT = (((1,), (1,)), ((), ()))


def place_of(group, share):
    device = lax.axis_index("seq")
    return lax.div(device, group), lax.rem(device, share), lax.div(lax.rem(device, group), share)


def run(kernel, out_shape, operands, scratch=(), flops=0, held=True, made=True):
    vmem = pl.BlockSpec(memory_space=pltpu.VMEM)
    home = pltpu.VMEM if held else pltpu.HBM
    moved = list(operands) + list(out_shape)
    operands = [pltpu.with_memory_space_constraint(a, home) for a in operands]
    return pl.pallas_call(
        kernel,
        out_shape=[pltpu.VMEM(a.shape, a.dtype) for a in out_shape] if made else out_shape,
        in_specs=[pl.BlockSpec(memory_space=home)] * len(operands),
        out_specs=[vmem] * len(out_shape),
        scratch_shapes=list(scratch),
        cost_estimate=pl.CostEstimate(
            flops=flops, bytes_accessed=sum(math.prod(a.shape) * a.dtype.itemsize for a in moved), transcendentals=0
        ),
        compiler_params=pltpu.CompilerParams(vmem_limit_bytes=VMEM_BYTES),
    )(*operands)


def columns_of(index, width=HEAD_SIZE):
    return pl.ds(pl.multiple_of(index * width, HEAD_SIZE), width)


def pack_kernel(place, queries, grad_out, keys, values, *refs):
    *parts, sems = refs
    rows = queries.shape[0]
    turns = len(parts) // 2
    heads = queries.shape[1] // HEAD_SIZE // turns
    moves = []
    for turn in range(turns):
        target = place[2] ^ turn
        moves.append((keys, target, parts[turn].at[:, :HEAD_SIZE]))
        moves.append((values, target, parts[turn].at[:, HEAD_SIZE:]))
    for turn in range(turns):
        target = place[2] ^ turn
        for base, source in ((0, queries), (heads, grad_out)):
            for head in range(heads):
                at = pl.ds((base + head) * rows, rows)
                moves.append((source, target * heads + head, parts[turns + turn].at[at]))
    copies = [
        pltpu.make_async_copy(source.at[:, columns_of(column)], target, sems.at[n])
        for n, (source, column, target) in enumerate(moves)
    ]
    for copy in copies:
        copy.start()
    for copy in copies:
        copy.wait()


def unpack_queries_kernel(place, *refs):
    parts, grad_queries = refs[:-1], refs[-1]
    for turn, part in enumerate(parts):
        grad_queries[:, columns_of(place[2] ^ turn, part.shape[1])] = part[...]


def by_eight(array):
    return array.reshape(-1, 8, array.shape[1])


def sweep(place, turns, query_grads, grad_qs, key_all, key_t, mix_all, dkey, dmix, work):
    rows, width = grad_qs[0].shape
    length = WINDOW
    span = length // rows
    lanes = 2 * HEAD_SIZE
    pairs = width // lanes
    group_at, parity, head_at = place
    inv_root = 1.0 / math.sqrt(HEAD_SIZE)
    log2_scale = inv_root * math.log2(math.e)
    score_refs, gprob_refs, low_refs, dscore_refs = work[0:2], work[2:4], work[4:6], work[6:8]
    fill = jnp.where(group_at == 0, NEG_FILL, 0.0).astype(jnp.float32)
    key_at = lax.broadcasted_iota(jnp.int32, (rows, lanes), 0)
    query_at = lax.broadcasted_iota(jnp.int32, (rows, lanes), 1) & (rows - 1)
    causal = key_at <= query_at
    stats = {}

    def places(n):
        step, pair = n // pairs, n % pairs
        number = block_at(place, turns[step], parity)
        return step, pair, number, pl.multiple_of(number * rows, rows)

    def stacked(step, base):
        return query_grads[step][base // HEAD_SIZE * rows : (base + lanes) // HEAD_SIZE * rows]

    def scores_stage(n):
        step, pair, number, first = places(n)
        seen = pl.ds(first, length + rows)
        scores = lax.dot_general(
            key_all[seen], stacked(step, pair * lanes), NT, preferred_element_type=jnp.float32
        )
        grads = lax.dot_general(
            mix_all[seen], stacked(step, width + pair * lanes), NT, preferred_element_type=jnp.float32
        )
        edge = jnp.where(causal, scores[length:], scores[:rows] + fill)
        score_refs[n % 2][:rows] = edge
        score_refs[n % 2][rows:] = scores[rows:length]
        gprob_refs[n % 2][:rows] = jnp.where(causal, grads[length:], grads[:rows])
        gprob_refs[n % 2][rows:] = grads[rows:length]
        peak = jnp.max(by_eight(edge), axis=0)
        for c in range(1, span):
            part = jnp.max(by_eight(scores[c * rows : (c + 1) * rows]), axis=0)
            peak = jnp.maximum(peak, part + jnp.where(number + c < span, fill, 0.0))
        stats[n] = jnp.max(peak, axis=0, keepdims=True) * log2_scale

    def softmax_stage(n):
        step, pair, number, first = places(n)
        peak = stats[n]
        scores, gprob, low, dscore = (refs[n % 2] for refs in (score_refs, gprob_refs, low_refs, dscore_refs))
        total = jnp.zeros((8, lanes), jnp.float32)
        delta = jnp.zeros((8, lanes), jnp.float32)
        for c in range(span):
            at = slice(c * rows, (c + 1) * rows)
            shift = -peak if c == 0 else jnp.where(number + c < span, fill, 0.0) - peak
            prob = jnp.exp2(scores[at] * log2_scale + shift)
            total = total + jnp.sum(by_eight(prob), axis=0)
            delta = delta + jnp.sum(by_eight(prob * gprob[at]), axis=0)
            low[at] = prob.astype(jnp.bfloat16)
        inverse = 1.0 / jnp.sum(total, axis=0, keepdims=True)
        delta = jnp.sum(delta, axis=0, keepdims=True) * inverse
        for c in range(span):
            at = slice(c * rows, (c + 1) * rows)
            dscore[at] = low[at] * (gprob[at] - delta).astype(jnp.bfloat16)
        zero = jnp.zeros((), jnp.bfloat16)
        for ref in (low, dscore):
            edge = ref[:rows]
            ref[length:] = jnp.where(causal, edge, zero)
            ref[:rows] = jnp.where(causal, zero, edge)
        stats[n] = inverse

    def gradient_stage(n):
        step, pair, number, first = places(n)
        seen = pl.ds(first, length + rows)
        inverse = stats[n]
        column = jnp.transpose(jnp.broadcast_to(inverse, (HEAD_SIZE, lanes)))
        query = (stacked(step, pair * lanes).astype(jnp.float32) * column).astype(jnp.bfloat16)
        grad = (stacked(step, width + pair * lanes).astype(jnp.float32) * column).astype(jnp.bfloat16)
        low, dscore = low_refs[n % 2], dscore_refs[n % 2]
        dmix[pl.ds(first + HALO, length + rows)] += jnp.dot(low[...], grad, preferred_element_type=jnp.float32)
        dkey[seen] += jnp.dot(dscore[...], query, preferred_element_type=jnp.float32)
        dquery = jnp.dot(key_t[:, seen], dscore[...], preferred_element_type=jnp.float32)
        dquery = jnp.transpose(dquery * (inverse * inv_root)).astype(jnp.bfloat16)
        for h in range(2):
            base = pair * lanes + h * HEAD_SIZE
            grad_qs[step][:, base : base + HEAD_SIZE] = dquery[h * rows : (h + 1) * rows]

    count = len(turns) * pairs
    for n in range(count + 2):
        if n < count:
            scores_stage(n)
        if 1 <= n <= count:
            softmax_stage(n - 1)
        if n >= 2:
            gradient_stage(n - 2)


def block_at(place, turn, core):
    return 2 * (place[2] ^ turn) + core


def attend_first_kernel(turns, place, *refs):
    kv_same, kv_other, old_same, old_other, halo, all_taps = refs[:6]
    query_grads, refs = refs[6 : 6 + turns], refs[6 + turns :]
    grad_qs, refs = refs[:turns], refs[turns:]
    key_all, key_t, mix_all, value_all, dkey, dmix, *work = refs
    blocks, rows = kv_same.shape[:2]
    span = 2 * blocks
    length = span * rows
    tap_count = all_taps.shape[0]
    parity = place[1]
    taps = all_taps[:, columns_of(place[2])]
    value_all[:HALO] = halo[...].astype(jnp.float32)
    for start, same, other in ((0, old_same, old_other), (span, kv_same, kv_other)):
        for turn in range(blocks):
            for source, core in ((same, parity), (other, 1 - parity)):
                first = pl.multiple_of((start + block_at(place, turn, core)) * rows, rows)
                key_all[pl.ds(first, rows)] = source[turn, :, :HEAD_SIZE]
                value_all[pl.ds(first + HALO, rows)] = source[turn, :, HEAD_SIZE:].astype(jnp.float32)
    for start in range(HALO, HALO + 2 * length, rows):
        mixed = taps[0:1] * value_all[start : start + rows]
        for index_k in range(1, tap_count):
            mixed = mixed + taps[index_k : index_k + 1] * value_all[start - index_k : start - index_k + rows]
        mix_all[start - HALO : start - HALO + rows] = mixed.astype(jnp.bfloat16)
    key_t[...] = jnp.transpose(key_all[...])
    dkey[...] = jnp.zeros_like(dkey)
    dmix[...] = jnp.zeros_like(dmix)
    sweep(place, range(turns), query_grads, grad_qs, key_all, key_t, mix_all, dkey, dmix, work)


def attend_last_kernel(scale, turns, place, *refs):
    all_taps, key_all, key_t, mix_all, value_all, dkey_before, dmix_before = refs[:7]
    query_grads, refs = refs[7 : 7 + turns], refs[7 + turns :]
    grad_qs, refs = refs[:turns], refs[turns:]
    send, keep_old, keep_own, tap_keep, dkey, dmix, *work = refs
    rows = grad_qs[0].shape[0]
    blocks = keep_old.shape[0] // rows
    span = 2 * blocks
    length = span * rows
    tap_count = all_taps.shape[0]
    parity = place[1]
    taps = all_taps[:, columns_of(place[2])]
    inv_root = 1.0 / math.sqrt(HEAD_SIZE)
    dkey[...] = dkey_before[...]
    dmix[...] = dmix_before[...]
    sweep(place, range(blocks - turns, blocks), query_grads, grad_qs, key_all, key_t, mix_all, dkey, dmix, work)

    def convolved(start, size):
        total = taps[0:1] * dmix[pl.ds(start, size)]
        for index_k in range(1, tap_count):
            total = total + taps[index_k : index_k + 1] * dmix[pl.ds(start + index_k, size)]
        return total

    for start, keep, base in ((0, keep_old, 0), (span, keep_own, blocks * rows)):
        for turn in range(blocks):
            for target, core, offset in ((keep, parity, 0), (send, 1 - parity, base)):
                first = pl.multiple_of((start + block_at(place, turn, core)) * rows, rows)
                at = slice(offset + turn * rows, offset + (turn + 1) * rows)
                target[at, :HEAD_SIZE] = (dkey[pl.ds(first, rows)] * inv_root).astype(target.dtype)
                target[at, HEAD_SIZE:] = convolved(first + HALO, rows).astype(target.dtype)
    note = slice(2 * blocks * rows, 2 * blocks * rows + HALO)
    send[note, HEAD_SIZE:] = convolved(0, HALO).astype(send.dtype)
    sums = [jnp.zeros((8, HEAD_SIZE), jnp.float32)] * tap_count
    for start in range(HALO, HALO + 2 * length, rows):
        grad = dmix[start : start + rows]
        for index_k in range(tap_count):
            sums[index_k] = sums[index_k] + jnp.sum(
                by_eight(grad * value_all[start - index_k : start - index_k + rows]), axis=0
            )
    tap_grads = jnp.concatenate([jnp.sum(total, axis=0, keepdims=True) for total in sums], axis=0) * scale
    low, high = tap_grads[:, : HEAD_SIZE // 2], tap_grads[:, HEAD_SIZE // 2 :]
    tap_keep[...] = jnp.where(parity == 0, low, high)
    theirs = jnp.where(parity == 0, high, low)
    upper = theirs.astype(send.dtype).astype(jnp.float32)
    theirs = jnp.concatenate([upper, theirs - upper], axis=0)
    theirs = jnp.concatenate([theirs, jnp.zeros((HALO - 2 * tap_count, HEAD_SIZE // 2), jnp.float32)], axis=0)
    theirs = jnp.concatenate([theirs, jnp.zeros_like(theirs)], axis=1)
    send[note, :HEAD_SIZE] = theirs.astype(send.dtype)


def on_device(queries, keys, values, conv_taps, grad_out):
    rows, width = queries.shape[1:]
    kv_width = keys.shape[2]
    tap_count = conv_taps.shape[0]
    kv_heads = kv_width // HEAD_SIZE
    group = WINDOW // rows
    share = group // kv_heads
    count = lax.axis_size("seq")
    planes = count // group
    own_width = width // kv_heads
    bf16, f32 = jnp.bfloat16, jnp.float32
    shape = jax.ShapeDtypeStruct
    plane, parity, head_at = place_of(group, share)

    def launch(kernel, out_shape, operands, **options):
        return run(lambda *refs: kernel(place_of(group, share), *refs), out_shape, operands, **options)

    def routed(array, distance, chosen=lambda i: True):
        route = [(i, i + distance) for i in range(count) if 0 <= i + distance < count and chosen(i)]
        return lax.ppermute(array, "seq", route)

    def flipped(array, bits):
        return lax.ppermute(array, "seq", [(i, i ^ bits) for i in range(count)])

    def after(others, *arrays):
        return lax.optimization_barrier((*arrays, *others))[: len(arrays)]

    def exchanged(parts):
        return [parts[0]] + [flipped(parts[turn], turn * share) for turn in range(1, kv_heads)]

    kv_shape = shape((rows, 2 * HEAD_SIZE), bf16)
    query_shape = shape((2 * own_width // HEAD_SIZE * rows, HEAD_SIZE), bf16)
    parts = launch(
        pack_kernel,
        [kv_shape] * kv_heads + [query_shape] * kv_heads,
        (queries[0], grad_out[0], keys[0], values[0]),
        scratch=[pltpu.SemaphoreType.DMA((2 * kv_heads * (1 + own_width // HEAD_SIZE),))],
        held=False,
    )
    kv_same = jnp.stack(exchanged(parts[:kv_heads]))
    old_same = routed(kv_same, group)
    query_grads = exchanged(after([kv_same], *parts[kv_heads:]))
    kv_same, old_same = lax.optimization_barrier((kv_same, old_same))
    old_other = flipped(old_same, 1)
    kv_other = flipped(kv_same, 1)
    last = lax.dynamic_index_in_dim(kv_same, head_at ^ (kv_heads - 1), 0, keepdims=False)
    reach = 2 * group - (share - 1)
    halo = routed(last[rows - HALO :, HEAD_SIZE:], reach, lambda i: i % share == share - 1)
    lanes = 2 * HEAD_SIZE
    group_rows = kv_heads * rows
    half = kv_heads - 1
    work = [pltpu.VMEM((WINDOW, lanes), f32)] * 4 + [pltpu.VMEM((WINDOW + rows, lanes), bf16)] * 4
    sums = [shape((2 * WINDOW, HEAD_SIZE), f32), shape((HALO + 2 * WINDOW + HALO, HEAD_SIZE), f32)]
    kept = [
        shape((2 * WINDOW, HEAD_SIZE), bf16),
        shape((HEAD_SIZE, 2 * WINDOW), bf16),
        shape((2 * WINDOW, HEAD_SIZE), bf16),
        shape((HALO + 2 * WINDOW, HEAD_SIZE), f32),
    ]
    *early, key_all, key_t, mix_all, value_all, dkey, dmix = launch(
        functools.partial(attend_first_kernel, half),
        [shape((rows, own_width), bf16)] * half + kept + sums,
        (kv_same, kv_other, old_same, old_other, halo, conv_taps, *query_grads[:half]),
        scratch=work,
    )
    scale = 1.0 / math.sqrt(rows * count * lax.axis_size("rep"))
    *late, send, keep_old, keep_own, tap_keep = launch(
        functools.partial(attend_last_kernel, scale, kv_heads - half),
        [shape((rows, own_width), bf16)] * (kv_heads - half)
        + [
            shape((2 * group_rows + HALO, lanes), bf16),
            shape((group_rows, lanes), bf16),
            shape((group_rows, lanes), bf16),
            shape((tap_count, HEAD_SIZE // 2), f32),
        ],
        (conv_taps, key_all, key_t, mix_all, value_all, dkey, dmix, *query_grads[half:]),
        scratch=[pltpu.VMEM(a.shape, a.dtype) for a in sums] + work,
    )
    got = flipped(send, 1)
    note = got[2 * group_rows :].astype(f32)
    old_sum = (keep_old.astype(f32) + got[:group_rows].astype(f32)).astype(bf16)
    note, *grad_q = after([old_sum], note, *early, *late)
    returned = routed(old_sum, -group)
    grad_q = exchanged(grad_q)
    halo, tap_grads = note[:, HEAD_SIZE:], note[:, : HEAD_SIZE // 2]
    tap_grads = tap_keep + (tap_grads[:tap_count] + tap_grads[tap_count : 2 * tap_count])
    short = planes == tap_count == 4
    if short:
        low, high = jnp.split(tap_grads, 2)
        mine, theirs = jnp.where(plane < 2, low, high), jnp.where(plane < 2, high, low)
        theirs = jnp.pad(theirs, ((0, 6), (0, HEAD_SIZE // 2)))
        note = flipped(jnp.concatenate([halo, theirs], axis=0), 2 * group)
        tap_grads = mine + note[HALO : HALO + 2, : HEAD_SIZE // 2]
        returned_halo = jnp.where(plane < 2, note[:HALO], 0.0)
    else:
        returned_halo = routed(halo, -2 * group)
    total = keep_own.astype(f32) + got[group_rows : 2 * group_rows].astype(f32) + returned.astype(f32)
    halo_block = jnp.pad(returned_halo, ((rows - HALO, 0), (HEAD_SIZE, 0)))
    owned = []
    for turn in range(kv_heads):
        mine = total[turn * rows : (turn + 1) * rows]
        owned.append((mine + jnp.where((head_at ^ turn) == kv_heads - 1, halo_block, 0.0)).astype(bf16))
    grad_q = after(owned, *grad_q)
    owned = exchanged(owned)
    (grad_queries,) = launch(unpack_queries_kernel, [shape((rows, width), bf16)], tuple(grad_q), made=False)

    def in_order(parts):
        heads = []
        for head in range(kv_heads):
            chosen = parts[0]
            for turn in range(1, kv_heads):
                chosen = jnp.where((head_at ^ turn) == head, parts[turn], chosen)
            heads.append(chosen)
        return jnp.concatenate(heads, axis=1)

    grad_keys = in_order([part[:, :HEAD_SIZE] for part in owned])
    grad_values = in_order([part[:, HEAD_SIZE:] for part in owned])
    if short:
        low, high = tap_grads[0], tap_grads[1]
        even = plane % 2 == 0
        grad_taps = jnp.where(even, low, high) + flipped(jnp.where(even, high, low), group)
    else:
        spread = jnp.zeros((tap_count, kv_width), f32)
        spread = lax.dynamic_update_slice(spread, tap_grads, (0, (2 * head_at + parity) * (HEAD_SIZE // 2)))
        grad_taps = jnp.sum(lax.all_to_all(spread.reshape(count, -1), "seq", 0, 0, tiled=True), axis=0)
    grad_taps = lax.psum(grad_taps, "rep")
    return grad_queries[None], grad_keys[None], grad_values[None], grad_taps


def solution(mesh):
    in_specs = (
        P("rep", "seq", None),
        P("rep", "seq", None),
        P("rep", "seq", None),
        P(),
        P("rep", "seq", None),
    )
    out_specs = (P("rep", "seq", None), P("rep", "seq", None), P("rep", "seq", None), P("seq"))
    return jax.shard_map(
        on_device, mesh=mesh, in_specs=in_specs, out_specs=out_specs, check_vma=False
    )
```
